32 devices in a mesh: groups: 2 (over y), gx: 4 (over z), gy: 4 (over x, core).
Axes of the slice: x: 2, y: 2, z: 4, core: 2. Of those that a mesh axis runs over, the one named last changes fastest.
Arguments:
- hidden: bfloat16 [128, 16384], P(('groups', 'gy'), 'gx'), parts along dimension 0, may hold values from -6 to 6
- w_query: bfloat16 [16384, 16384], P('gx', 'gy'), may hold values from -0.046875 to 0.046875
- w_key: bfloat16 [16384, 1024], P('gx', 'gy'), may hold values from -0.1875 to 0.1875
- w_value: bfloat16 [16384, 1024], P('gx', 'gy'), may hold values from -0.1875 to 0.1875
- w_out: bfloat16 [16384, 16384], P('gy', 'gx'), may hold values from -0.046875 to 0.046875
- cache_keys: bfloat16 [128, 512, 1024], P(('groups', 'gx', 'gy')), parts along dimension 0, may hold values from -756 to 756, as said below
- cache_values: bfloat16 [128, 512, 1024], P(('groups', 'gx', 'gy')), parts along dimension 0, may hold values from -24 to 24
- lengths: int32 [128], P(('groups', 'gx', 'gy')), parts along dimension 0, may hold values from 256 to 512, as said below
Outputs:
- attended: bfloat16 [128, 16384], P(('groups', 'gy'), 'gx'), parts along dimension 0
The draws below stay inside these ranges and needn't reach their ends.
There are 2 independent parts, one for each index of `groups`. The reference program is written for one: setup_inputs(seed, part) draws one part's arguments, and reference() takes and returns one part's arrays. A program takes and returns all parts, laid end to end along the dimension named above; an argument that names none is the same for every part. Nothing has to cross between parts.
Inputs may be any that keep to these rules, and one draw needn't show every extreme that they name: The new token sits at position lengths[b] of row b. `cache_keys`: keys already carry their rotary embedding.
All inputs are finite; a program needn't handle non-finite values.
Results may differ from the reference program's by a relative error of at most 0.0045.
The reference program's roundings to bfloat16 on the way (of `heads_out`) count: a program that leaves them out, or rounds other values in their place, can miss the bound.
Values may be sent and summed in bfloat16 or wider, within the bound.
No kernel may reach another device: no remote copies, remote signals or barrier semaphores. Data moves between devices by JAX's collectives and lax.ppermute only.
A program may use at most 192 MiB of HBM per device.

```python
import jax
import jax.numpy as jnp
from jax import lax

D = 16384
KV = 8
HD = 128
CACHE = 512
GROUP = 16
QW = 16384
KW = 1024
ROWS = 64


def draw_cache_keys(key, part):
    key = jax.random.fold_in(key, 11)
    base = jnp.clip(jax.random.normal(key, (ROWS, CACHE, KV * HD), jnp.float32), -6.0, 6.0)
    return (base * 1.8).astype(jnp.bfloat16)


def draw_lengths(key, part):
    key = jax.random.fold_in(key, 23)
    key_values, key_longest, key_offset = jax.random.split(key, 3)
    values = jax.random.randint(key_values, (ROWS,), CACHE // 2, CACHE + 1, dtype=jnp.int32)
    longest = jax.random.randint(key_longest, (), 0, ROWS, dtype=jnp.int32)
    shortest = (longest + 1 + jax.random.randint(key_offset, (), 0, ROWS - 1, dtype=jnp.int32)) % ROWS
    values = values.at[longest].set(CACHE)
    values = values.at[shortest].set(CACHE // 2)
    return values


def block_levels(own_key, dims, shards, low, top_value):
    level, own = 1.0, jax.random.fold_in(own_key, 6)
    for axis_at, blocks in shards:
        draws = jnp.exp(jax.random.uniform(jax.random.fold_in(own, axis_at), (blocks,), jnp.float32, low / len(shards), top_value / len(shards)))
        level = level * jnp.repeat(draws, dims[axis_at] // blocks).reshape([-1 if axis == axis_at else 1 for axis in range(len(dims))])
    return level


def noise(own_key, shape, deviation, limit, pieces=(), kind=jnp.bfloat16):
    drawn = jax.random.normal(own_key, shape, jnp.float32) * deviation
    if len(pieces) > 0:
        drawn = block_levels(own_key, shape, pieces, -0.22, 0.18) * drawn
    return jnp.clip(drawn, min=-limit, max=limit).astype(kind)


def setup_inputs(seed: int = 0, part: int = 0) -> dict:
    seeds = jax.random.split(jax.random.key(seed), 9)
    part_keys = jax.random.split(jax.random.fold_in(seeds[8], part), 9)
    return {
        "hidden": noise(part_keys[0], (ROWS, D), 1.0, 6.0, ((0, 4), (1, 4))),
        "w_query": noise(seeds[1], (D, QW), D ** -0.5, 0.046875, ((0, 4), (1, 4))),
        "w_key": noise(seeds[2], (D, KW), (D // 16) ** -0.5, 0.1875, ((0, 4), (1, 4))),
        "w_value": noise(seeds[3], (D, KW), (D // 16) ** -0.5, 0.1875, ((0, 4), (1, 4))),
        "w_out": noise(seeds[4], (QW, D), QW ** -0.5, 0.046875, ((0, 4), (1, 4))),
        "cache_keys": draw_cache_keys(jax.random.fold_in(jax.random.fold_in(seeds[8], part), 71), part),
        "cache_values": noise(part_keys[6], (ROWS, CACHE, KW), 4.0, 24.0, ((0, 16),)),
        "lengths": draw_lengths(jax.random.fold_in(jax.random.fold_in(seeds[8], part), 71), part),
    }


def rotate(vectors, positions):
    half = vectors.shape[-1] // 2
    frequency = 500000.0 ** (-(jnp.arange(half, dtype=jnp.float32) * 2.0) / vectors.shape[-1])
    angles = positions.astype(jnp.float32) * frequency
    cosine = jnp.cos(angles)
    sine_part = jnp.sin(angles)
    first_half = vectors[..., :half]
    second_half = vectors[..., half:]
    return jnp.concatenate([first_half * cosine - second_half * sine_part, second_half * cosine + first_half * sine_part], axis=-1)

def attend_row(operands):
    query_row, key_row, value_row, past_keys, past_values, length = operands
    score_scale = 1.0 / jnp.sqrt(jnp.float32(HD))
    queries = rotate(query_row.astype(jnp.float32).reshape(KV, GROUP, HD), length).astype(jnp.bfloat16)
    key_rot = rotate(key_row.astype(jnp.float32).reshape(KV, HD), length).astype(jnp.bfloat16)
    value_new = value_row.reshape(KV, HD)
    keys_all = past_keys.reshape(CACHE, KV, HD)
    values_all = past_values.reshape(CACHE, KV, HD)
    scores = jnp.einsum('ghd,tgd->ght', queries.astype(jnp.float32), keys_all.astype(jnp.float32)) * score_scale
    visible = jnp.arange(CACHE, dtype=jnp.int32) < length
    scores = jnp.where(visible[None, None, :], scores, -jnp.inf)
    own_score = jnp.einsum('ghd,gd->gh', queries.astype(jnp.float32), key_rot.astype(jnp.float32)) * score_scale
    highest = jnp.maximum(lax.optimization_barrier(jnp.max(scores, axis=-1)), own_score)
    weights = jnp.exp(scores - highest[..., None])
    own_weight = jnp.exp(own_score - highest)
    denominator = lax.optimization_barrier(jnp.sum(weights, axis=-1)) + own_weight
    weights_low = weights.astype(jnp.bfloat16)
    own_low = own_weight.astype(jnp.bfloat16)
    mixture = jnp.einsum('ght,tgd->ghd', weights_low.astype(jnp.float32), values_all.astype(jnp.float32))
    mixture = mixture + own_low.astype(jnp.float32)[..., None] * value_new.astype(jnp.float32)[:, None, :]
    return (mixture / denominator[..., None]).astype(jnp.bfloat16).reshape(QW)

def reference(hidden, w_query, w_key, w_value, w_out, cache_keys, cache_values, lengths):
    queries = jnp.dot(hidden, w_query, preferred_element_type=jnp.float32).astype(jnp.bfloat16)
    keys_new = jnp.dot(hidden, w_key, preferred_element_type=jnp.float32).astype(jnp.bfloat16)
    values_new = jnp.dot(hidden, w_value, preferred_element_type=jnp.float32).astype(jnp.bfloat16)
    heads_out = lax.map(attend_row, (queries, keys_new, values_new, cache_keys, cache_values, lengths))
    return jnp.dot(heads_out, w_out, preferred_element_type=jnp.float32).astype(jnp.bfloat16)
```

```python
import functools

import jax
import jax.numpy as jnp
import numpy as np
from jax import lax
from jax.experimental import pallas as pl
from jax.experimental.pallas import tpu as pltpu
from jax.sharding import PartitionSpec as P

HD = 128
MIB = 1 << 20
F32 = jnp.float32
BF16 = jnp.bfloat16


def swap(x, axis, offset):
    n = lax.axis_size(axis)
    return lax.ppermute(x, axis, [(i, i ^ offset) for i in range(n)])


def bit_list(n):
    return [1 << b for b in range(n.bit_length() - 1)]


def halves_order(n):
    bits = bit_list(n)
    out = []
    for position in range(n):
        k = 0
        for level, bit in enumerate(bits):
            if position >> (len(bits) - 1 - level) & 1:
                k |= bit
        out.append(k)
    return np.array(out)


def one_hot(columns, size):
    return (columns[:, None] == jnp.arange(size, dtype=jnp.int32)[None, :]).astype(BF16)


def qkv_kernel(count, half, *refs):
    blocks, (perm, wq, wk, wv, keep, send, gathered) = refs[:count], refs[count:]
    step = pl.program_id(0)
    depth, query_cols = wq.shape

    @pl.when(step == 0)
    def _():
        rows = blocks[0].shape[0]
        for k in range(count):
            gathered[k * rows : (k + 1) * rows, :] = blocks[k][...]

    here = pl.ds(pl.multiple_of(step * depth, depth), depth)
    x = jnp.dot(perm[...], gathered[:, here], preferred_element_type=F32).astype(BF16)
    at = 0
    for w in (wq, wk, wv):
        width = w.shape[1]
        product = jnp.dot(x, w[...], preferred_element_type=F32)
        cols = slice(at, at + width)

        @pl.when(step == 0)
        def _():
            keep[:, cols] = product[:half]
            send[:, cols] = product[half:]

        @pl.when(step > 0)
        def _():
            keep[:, cols] += product[:half]
            send[:, cols] += product[half:]

        at += width


def project(blocks, perm, w_query, w_key, w_value, chunk, chunks):
    rows = perm.shape[0]
    depth_all = w_query.shape[0]
    qc, kc = w_query.shape[1] // chunks, w_key.shape[1] // chunks
    depth = min(512, depth_all)
    width = qc + 2 * kc
    out = jax.ShapeDtypeStruct((rows // 2, width), F32)
    whole = lambda a: pl.BlockSpec(a.shape, lambda j: (0, 0))
    return pl.pallas_call(
        functools.partial(qkv_kernel, len(blocks), rows // 2),
        name=f"project_{chunk}",
        grid=(depth_all // depth,),
        in_specs=[whole(b) for b in blocks]
        + [
            whole(perm),
            pl.BlockSpec((depth, qc), lambda j: (j, chunk)),
            pl.BlockSpec((depth, kc), lambda j: (j, chunk)),
            pl.BlockSpec((depth, kc), lambda j: (j, chunk)),
        ],
        out_specs=[pl.BlockSpec((rows // 2, width), lambda j: (0, 0))] * 2,
        out_shape=[out, out],
        scratch_shapes=[pltpu.VMEM((rows, depth_all), BF16)],
        compiler_params=pltpu.CompilerParams(vmem_limit_bytes=32 * MIB),
        cost_estimate=pl.CostEstimate(
            flops=2 * rows * depth_all * width, bytes_accessed=2 * depth_all * width, transcendentals=0
        ),
    )(*blocks, perm, w_query, w_key, w_value)


def attend_kernel(count, heads, groups, lengths, *refs):
    blocks, (cosine, sine, keys, values, keep, send, staged, mixed) = refs[:count], refs[count:]
    rows = blocks[0].shape[0]
    slots = keys.shape[1]
    query_cols = heads * HD
    scale = 1.0 / jnp.sqrt(jnp.float32(HD))
    cos, sin = cosine[...], sine[...]

    def rotated(u):
        return u * cos + pltpu.roll(u, HD // 2, 1) * sin

    for k in range(count):
        block = blocks[k]
        group = groups[k]
        lanes = pl.ds(pl.multiple_of(group * HD, HD), HD)
        for h in range(heads):
            u = block[:, h * HD : (h + 1) * HD].astype(F32)
            staged[:, h, :] = rotated(u)
        key_rot = rotated(block[:, query_cols : query_cols + HD].astype(F32)).astype(BF16).astype(F32)
        value_new = block[:, query_cols + HD :].astype(F32)
        for r in range(rows):
            q = staged[r].astype(BF16)
            scores = (
                lax.dot_general(
                    q, keys[r, :, lanes], (((1,), (1,)), ((), ())), preferred_element_type=F32
                )
                * scale
            )
            slot = lax.broadcasted_iota(jnp.int32, scores.shape, 1)
            scores = jnp.where(slot < lengths[r], scores, -jnp.inf)
            own = jnp.sum(q.astype(F32) * key_rot[r : r + 1], axis=1, keepdims=True) * scale
            highest = jnp.maximum(jnp.max(scores, axis=1, keepdims=True), own)
            weights = jnp.exp(scores - highest)
            own_weight = jnp.exp(own - highest)
            denominator = jnp.sum(weights, axis=1, keepdims=True) + own_weight
            mixture = jnp.dot(weights.astype(BF16), values[r, :, lanes], preferred_element_type=F32)
            mixture = mixture + own_weight.astype(BF16).astype(F32) * value_new[r : r + 1]
            mixed[r] = mixture / denominator
        target = keep if k < count // 2 else send
        at = (k % (count // 2)) * rows
        for h in range(heads):
            target[at : at + rows, h * HD : (h + 1) * HD] = mixed[:, h, :].astype(BF16)


def attend(blocks, groups, lengths, cosine, sine, cache_keys, cache_values, chunk):
    rows, width = blocks[0].shape
    heads = (width - 2 * HD) // HD
    count = len(blocks)
    out = jax.ShapeDtypeStruct((count // 2 * rows, heads * HD), BF16)
    smem = pl.BlockSpec(memory_space=pltpu.SMEM)
    vmem = pl.BlockSpec(memory_space=pltpu.VMEM)
    return pl.pallas_call(
        functools.partial(attend_kernel, count, heads),
        name=f"attend_{chunk}",
        in_specs=[smem, smem] + [vmem] * (count + 4),
        out_specs=[vmem, vmem],
        out_shape=[out, out],
        scratch_shapes=[pltpu.VMEM((rows, heads, HD), F32), pltpu.VMEM((rows, heads, HD), F32)],
        compiler_params=pltpu.CompilerParams(vmem_limit_bytes=8 * MIB),
    )(groups, lengths, *blocks, cosine, sine, cache_keys, cache_values)


def out_kernel(count, pieces, half, *refs):
    blocks, (perm, w, keep, send, gathered) = refs[: count * pieces], refs[count * pieces :]
    step = pl.program_id(0)
    depth = w.shape[0]

    @pl.when(step == 0)
    def _():
        rows, width = blocks[0].shape
        for c in range(pieces):
            for k in range(count):
                gathered[k * rows : (k + 1) * rows, c * width : (c + 1) * width] = blocks[c * count + k][...]

    here = pl.ds(pl.multiple_of(step * depth, depth), depth)
    x = jnp.dot(perm[...], gathered[:, here], preferred_element_type=F32).astype(BF16)
    product = jnp.dot(x, w[...], preferred_element_type=F32)

    @pl.when(step == 0)
    def _():
        keep[...] = product[:half]
        send[...] = product[half:]

    @pl.when(step > 0)
    def _():
        keep[...] += product[:half]
        send[...] += product[half:]


def out_project(blocks, pieces, perm, w_out):
    rows = perm.shape[0]
    depth_all, cols = w_out.shape
    depth = min(512, depth_all)
    out = jax.ShapeDtypeStruct((rows // 2, cols), F32)
    whole = lambda a: pl.BlockSpec(a.shape, lambda j: (0, 0))
    return pl.pallas_call(
        functools.partial(out_kernel, len(blocks) // pieces, pieces, rows // 2),
        name="project_out",
        grid=(depth_all // depth,),
        in_specs=[whole(b) for b in blocks]
        + [whole(perm), pl.BlockSpec((depth, cols), lambda j: (j, 0))],
        out_specs=[pl.BlockSpec((rows // 2, cols), lambda j: (0, 0))] * 2,
        out_shape=[out, out],
        scratch_shapes=[pltpu.VMEM((rows, depth_all), BF16)],
        compiler_params=pltpu.CompilerParams(vmem_limit_bytes=32 * MIB),
        cost_estimate=pl.CostEstimate(
            flops=2 * rows * depth_all * cols, bytes_accessed=2 * depth_all * cols, transcendentals=0
        ),
    )(*blocks, perm, w_out)


def local(hidden, w_query, w_key, w_value, w_out, cache_keys, cache_values, lengths):
    nz, ny = lax.axis_size("gx"), lax.axis_size("gy")
    z, y = lax.axis_index("gx"), lax.axis_index("gy")
    rows_dev = lengths.shape[0]
    rows = rows_dev * nz * ny
    rows_y, rows_z = rows // ny, rows // nz
    chunks = w_key.shape[1] // HD
    high_first = list(reversed(bit_list(ny)))

    kz, ky, i = np.meshgrid(halves_order(nz), np.arange(ny), np.arange(rows_dev), indexing="ij")
    kz, ky, i = (jnp.asarray(a.reshape(-1), jnp.int32) for a in (kz, ky, i))
    row = ((kz ^ z) * ny + (ky ^ y)) * rows_dev + i
    perm_in = one_hot(((row // rows_y) ^ y) * rows_y + row % rows_y, rows)
    ko, t = np.meshgrid(halves_order(ny), np.arange(rows_y), indexing="ij")
    ko, t = (jnp.asarray(a.reshape(-1), jnp.int32) for a in (ko, t))
    row = (ko ^ y) * rows_y + t
    from_z, rest = row // rows_z, row % rows_z
    perm_out = one_hot(
        ((from_z ^ z) * ny + ((rest // rows_dev) ^ y)) * rows_dev + rest % rows_dev, rows
    )

    frequency = 500000.0 ** (-(jnp.arange(HD // 2, dtype=F32) * 2.0) / HD)
    angles = lengths.astype(F32)[:, None] * frequency[None, :]
    cosine, sine = jnp.cos(angles), jnp.sin(angles)
    cosine = jnp.concatenate([cosine, cosine], axis=1)
    sine = jnp.concatenate([-sine, sine], axis=1)

    blocks = {0: hidden}
    for bit in high_first:
        blocks.update({k | bit: swap(b, "gy", bit) for k, b in list(blocks.items())})
    blocks = [blocks[k] for k in range(ny)]

    received = []
    for c in range(chunks):
        keep, send = project(blocks, perm_in, w_query, w_key, w_value, c, chunks)
        for bit in bit_list(nz):
            if bit > 1:
                middle = total.shape[0] // 2
                keep, send = total[:middle], total[middle:]
            total = keep + swap(send, "gx", bit)
        parts = {0: total.astype(BF16)}
        for bit in high_first:
            middle = parts[0].shape[0] // 2
            fresh = {}
            for k, part in parts.items():
                fresh[k] = part[:middle]
                fresh[k | bit] = swap(part[middle:], "gy", bit)
            parts = fresh
        groups = (jnp.arange(ny, dtype=jnp.int32) ^ y) * chunks + c
        keep, send = attend(
            [parts[k] for k in range(ny)], groups, lengths, cosine, sine, cache_keys, cache_values, c
        )
        first = high_first[0]
        parts = {0: keep, first: swap(send, "gy", first)}
        for bit in high_first[1:]:
            middle = parts[0].shape[0] // 2
            fresh = {}
            for k, part in parts.items():
                fresh[k] = part[:middle]
                fresh[k | bit] = swap(part[middle:], "gy", bit)
            parts = fresh
        mine = jnp.concatenate([parts[k] for k in range(ny)], axis=0)
        received += [mine] + [swap(mine, "gx", k) for k in range(1, nz)]

    keep, send = out_project(received, chunks, perm_out, w_out)
    for bit in bit_list(ny):
        if bit > 1:
            middle = total.shape[0] // 2
            keep, send = total[:middle], total[middle:]
        total = keep + swap(send, "gy", bit)
    return total.astype(BF16)


def solution(mesh):
    placed = (
        P(("groups", "gy"), "gx"),
        P("gx", "gy"),
        P("gx", "gy"),
        P("gx", "gy"),
        P("gy", "gx"),
        P(("groups", "gx", "gy"), None, None),
        P(("groups", "gx", "gy"), None, None),
        P(("groups", "gx", "gy")),
    )
    return jax.shard_map(
        local, mesh=mesh, in_specs=placed, out_specs=P(("groups", "gy"), "gx"), check_vma=False
    )
```

```python
import functools

import jax
import jax.numpy as jnp
import numpy as np
from jax import lax
from jax.experimental import pallas as pl
from jax.experimental.pallas import tpu as pltpu
from jax.sharding import PartitionSpec as P

HD = 128
MIB = 1 << 20
F32 = jnp.float32
BF16 = jnp.bfloat16


def swap(x, axis, offset):
    n = lax.axis_size(axis)
    return lax.ppermute(x, axis, [(i, i ^ offset) for i in range(n)])


def bit_list(n):
    return [1 << b for b in range(n.bit_length() - 1)]


def halves_order(n):
    bits = bit_list(n)
    out = []
    for position in range(n):
        k = 0
        for level, bit in enumerate(bits):
            if position >> (len(bits) - 1 - level) & 1:
                k |= bit
        out.append(k)
    return np.array(out)


def one_hot(columns, size):
    return (columns[:, None] == jnp.arange(size, dtype=jnp.int32)[None, :]).astype(BF16)


def in_hbm(x):
    return pltpu.with_memory_space_constraint(x, pltpu.HBM)


def in_vmem(x):
    return pltpu.with_memory_space_constraint(x, pltpu.VMEM)


ANYWHERE = pl.BlockSpec(memory_space=pl.ANY)
IN_VMEM = pl.BlockSpec(memory_space=pltpu.VMEM)
IN_SMEM = pl.BlockSpec(memory_space=pltpu.SMEM)


def row_pieces(rows, wanted=8):
    pieces = wanted
    while rows % pieces or (rows >= 16 * pieces and (rows // pieces) % 16):
        pieces //= 2
    return pieces


def copy_pieces(source, target, sems):
    pieces = row_pieces(target.shape[0])
    step = target.shape[0] // pieces

    def piece(n):
        at = pl.ds(pl.multiple_of(n * step, step), step)
        return pltpu.make_async_copy(source.at[at], target.at[at], sems.at[n])

    return pieces, piece


def start_copies(*copies):
    for pieces, piece in copies:
        pl.loop(0, pieces)(lambda n: piece(n).start())


def wait_copies(*copies):
    for pieces, piece in copies:
        pl.loop(0, pieces)(lambda n: piece(n).wait())


def fetch_kernel(plan, count, *refs):
    sources, targets, sems = refs[:count], refs[count:-1], refs[-1]
    copies = [
        copy_pieces(sources[source].at[window], targets[target].at[place], sems.at[n])
        for n, (source, window, target, place) in enumerate(plan)
    ]
    start_copies(*copies)
    wait_copies(*copies)


def fetch(name, arrays, shapes, plan):
    return pl.pallas_call(
        functools.partial(fetch_kernel, plan, len(arrays)),
        name=name,
        in_specs=[ANYWHERE] * len(arrays),
        out_specs=[IN_VMEM] * len(shapes),
        out_shape=[pltpu.VMEM(shape, BF16) for shape in shapes],
        scratch_shapes=[pltpu.SemaphoreType.DMA((len(plan), 8))],
        compiler_params=pltpu.CompilerParams(vmem_limit_bytes=MIB),
        cost_estimate=pl.CostEstimate(
            flops=0, bytes_accessed=2 * sum(int(np.prod(shape)) for shape in shapes), transcendentals=0
        ),
    )(*[in_hbm(a) for a in arrays])


def after(x, *done):
    return lax.optimization_barrier((x, *done))[0]


def tile_of(width, wanted=512):
    return wanted if width % wanted == 0 else width


def first_kernel(count, half, chunk_cols, ahead, *refs):
    blocks, refs = refs[:count], refs[count:]
    perm, wq, wkv, rest = refs[:4]
    keep, send, x = refs[4:7]
    gathered, sems = refs[-2:]
    copies = []
    if ahead:
        window = rest.at[pl.ds(0, refs[7].shape[0]), pl.ds(chunk_cols, chunk_cols)]
        copies = [copy_pieces(window, refs[7], sems)]
    start_copies(*copies)
    rows = blocks[0].shape[0]
    for k in range(count):
        gathered[k * rows : (k + 1) * rows, :] = blocks[k][...]
    width = x.shape[1]
    tile = tile_of(width)
    for at in range(0, width, tile):
        x[:, at : at + tile] = jnp.dot(
            perm[...], gathered[:, at : at + tile], preferred_element_type=F32
        ).astype(BF16)
    at = 0
    for w in (wq, wkv):
        tile = tile_of(w.shape[1])
        for n in range(0, w.shape[1], tile):
            product = jnp.dot(x[...], w[:, n : n + tile], preferred_element_type=F32)
            keep[:, at + n : at + n + tile] = product[:half]
            send[:, at + n : at + n + tile] = product[half:]
        at += w.shape[1]
    wait_copies(*copies)


def project_first(blocks, perm, w_first, w_kv, w_query, chunks):
    rows = perm.shape[0]
    depth, qc = w_first.shape
    width = qc + 2 * HD
    ahead = chunks > 1
    out = jax.ShapeDtypeStruct((rows // 2, width), F32)
    return pl.pallas_call(
        functools.partial(first_kernel, len(blocks), rows // 2, qc, ahead),
        name="project_first",
        in_specs=[IN_VMEM] * (len(blocks) + 3) + [ANYWHERE],
        out_specs=[IN_VMEM] * (4 if ahead else 3),
        out_shape=[out, out, pltpu.VMEM((rows, depth), BF16)]
        + ([pltpu.VMEM((depth * 3 // 4, qc), BF16)] if ahead else []),
        scratch_shapes=[pltpu.VMEM((rows, depth), BF16), pltpu.SemaphoreType.DMA((8,))],
        compiler_params=pltpu.CompilerParams(vmem_limit_bytes=6 * MIB),
        cost_estimate=pl.CostEstimate(
            flops=2 * rows * depth * width, bytes_accessed=4 * depth * width, transcendentals=0
        ),
    )(*blocks, perm, in_vmem(w_first), in_vmem(w_kv), in_hbm(w_query))


def next_kernel(half, chunk, more, extra, x, w_early, wkv, rest, *refs):
    sources, refs = refs[:extra], refs[extra:]
    keep, send = refs[:2]
    late, sems = refs[-2:]
    early_rows, qc = w_early.shape
    late_rows = late.shape[0]
    copies = [copy_pieces(rest.at[pl.ds(early_rows, late_rows), pl.ds(chunk * qc, qc)], late, sems.at[0])]
    if more:
        copies.append(
            copy_pieces(rest.at[pl.ds(0, early_rows), pl.ds((chunk + 1) * qc, qc)], refs[2], sems.at[1])
        )
    for n in range(extra):
        copies.append(copy_pieces(sources[n], refs[2 + more + n], sems.at[2 + n]))
    start_copies(*copies)
    tile = tile_of(qc)
    for n in range(0, qc, tile):
        product = jnp.dot(x[:, :early_rows], w_early[:, n : n + tile], preferred_element_type=F32)
        keep[:, n : n + tile] = product[:half]
        send[:, n : n + tile] = product[half:]
    product = jnp.dot(x[...], wkv[...], preferred_element_type=F32)
    keep[:, qc:] = product[:half]
    send[:, qc:] = product[half:]
    wait_copies(copies[0])
    for n in range(0, qc, tile):
        product = jnp.dot(x[:, early_rows:], late[:, n : n + tile], preferred_element_type=F32)
        keep[:, n : n + tile] += product[:half]
        send[:, n : n + tile] += product[half:]
    wait_copies(*copies[1:])


def project_next(x, w_early, w_kv, w_query, chunk, chunks, fetched=()):
    rows, depth = x.shape
    qc = w_early.shape[1]
    width = qc + 2 * HD
    more = chunk + 1 < chunks
    out = jax.ShapeDtypeStruct((rows // 2, width), F32)
    return pl.pallas_call(
        functools.partial(next_kernel, rows // 2, chunk, more, len(fetched)),
        name=f"project_next_{chunk}",
        in_specs=[IN_VMEM] * 3 + [ANYWHERE] * (1 + len(fetched)),
        out_specs=[IN_VMEM] * (2 + more + len(fetched)),
        out_shape=[out, out]
        + ([pltpu.VMEM(w_early.shape, BF16)] if more else [])
        + [pltpu.VMEM(a.shape, a.dtype) for a in fetched],
        scratch_shapes=[
            pltpu.VMEM((depth - w_early.shape[0], qc), BF16),
            pltpu.SemaphoreType.DMA((2 + len(fetched), 8)),
        ],
        compiler_params=pltpu.CompilerParams(vmem_limit_bytes=10 * MIB),
        cost_estimate=pl.CostEstimate(
            flops=2 * rows * depth * width, bytes_accessed=4 * depth * width, transcendentals=0
        ),
    )(x, in_vmem(w_early), in_vmem(w_kv), in_hbm(w_query), *[in_hbm(a) for a in fetched])


def attend_kernel(count, heads, groups, lengths, *refs):
    blocks, (cosine, sine, keys, values, keep, send) = refs[:count], refs[count : count + 6]
    packed, staged, scores, weights_low, mixed = refs[count + 6 :]
    rows = blocks[0].shape[0]
    pairs = count * rows
    slots = keys.shape[1]
    query_cols = heads * HD
    scale = 1.0 / jnp.sqrt(jnp.float32(HD))
    cos, sin = cosine[...], sine[...]

    def rotated(u):
        return u * cos + pltpu.roll(u, HD // 2, 1) * sin

    for k in range(count):
        packed[k * rows : (k + 1) * rows, :] = blocks[k][...].astype(F32)
    for h in range(heads):
        staged[:, h, :] = rotated(packed[:, h * HD : (h + 1) * HD])
    key_rot = rotated(packed[:, query_cols : query_cols + HD]).astype(BF16).astype(F32)
    slot = lax.broadcasted_iota(jnp.int32, (heads, slots), 1)

    def lanes(k):
        return pl.ds(pl.multiple_of(groups[k] * HD, HD), HD)

    for p in range(pairs):
        k, r = divmod(p, rows)
        scores[p] = lax.dot_general(
            staged[p].astype(BF16), keys[r, :, lanes(k)], (((1,), (1,)), ((), ())), preferred_element_type=F32
        )
    owns, denominators = [], []
    for p in range(pairs):
        r = p % rows
        q = staged[p].astype(BF16).astype(F32)
        masked = jnp.where(slot < lengths[r], scores[p] * scale, -jnp.inf)
        own = jnp.sum(q * key_rot[p : p + 1], axis=1, keepdims=True) * scale
        highest = jnp.maximum(jnp.max(masked, axis=1, keepdims=True), own)
        weights = jnp.exp(masked - highest)
        own_weight = jnp.exp(own - highest)
        denominators.append(jnp.sum(weights, axis=1, keepdims=True) + own_weight)
        owns.append(own_weight.astype(BF16).astype(F32))
        weights_low[p] = weights.astype(BF16)
    for p in range(pairs):
        k, r = divmod(p, rows)
        mixture = jnp.dot(weights_low[p], values[r, :, lanes(k)], preferred_element_type=F32)
        mixture = mixture + owns[p] * packed[p : p + 1, query_cols + HD :]
        mixed[p] = mixture / denominators[p]
    half = pairs // 2
    for h in range(heads):
        low = mixed[:, h, :].astype(BF16)
        keep[:, h * HD : (h + 1) * HD] = low[:half]
        send[:, h * HD : (h + 1) * HD] = low[half:]


def attend(blocks, groups, lengths, cosine, sine, cache_keys, cache_values, chunk):
    rows, width = blocks[0].shape
    heads = (width - 2 * HD) // HD
    count = len(blocks)
    pairs = count * rows
    slots = cache_keys.shape[1]
    out = jax.ShapeDtypeStruct((pairs // 2, heads * HD), BF16)
    return pl.pallas_call(
        functools.partial(attend_kernel, count, heads),
        name=f"attend_{chunk}",
        in_specs=[IN_SMEM, IN_SMEM] + [IN_VMEM] * (count + 4),
        out_specs=[IN_VMEM, IN_VMEM],
        out_shape=[out, out],
        scratch_shapes=[
            pltpu.VMEM((pairs, width), F32),
            pltpu.VMEM((pairs, heads, HD), F32),
            pltpu.VMEM((pairs, heads, slots), F32),
            pltpu.VMEM((pairs, heads, slots), BF16),
            pltpu.VMEM((pairs, heads, HD), F32),
        ],
        compiler_params=pltpu.CompilerParams(vmem_limit_bytes=8 * MIB),
        cost_estimate=pl.CostEstimate(
            flops=4 * pairs * heads * HD * slots, bytes_accessed=4 * rows * slots * count * HD, transcendentals=0
        ),
    )(groups, lengths, *blocks, cosine, sine, in_vmem(cache_keys), in_vmem(cache_values))


def gather_rows(blocks, perm, gathered):
    rows = blocks[0].shape[0]
    for k, block in enumerate(blocks):
        gathered[k * rows : (k + 1) * rows, :] = block[...]
    return jnp.dot(perm[...], gathered[...], preferred_element_type=F32).astype(BF16)


def early_kernel(count, *refs):
    blocks, (perm, w, total, gathered) = refs[:count], refs[count:]
    x = gather_rows(blocks, perm, gathered)
    width = total.shape[1]
    tile = tile_of(width)
    for n in range(0, width, tile):
        cols = slice(n, n + tile)
        total[:, cols] = jnp.dot(x, w[:, cols], preferred_element_type=F32)


def out_early(blocks, perm, w, chunk):
    rows = perm.shape[0]
    size, width = w.shape
    return pl.pallas_call(
        functools.partial(early_kernel, len(blocks)),
        name=f"out_early_{chunk}",
        in_specs=[IN_VMEM] * (len(blocks) + 2),
        out_specs=IN_VMEM,
        out_shape=pltpu.VMEM((rows, width), F32),
        scratch_shapes=[pltpu.VMEM((rows, size), BF16)],
        compiler_params=pltpu.CompilerParams(vmem_limit_bytes=6 * MIB),
        cost_estimate=pl.CostEstimate(
            flops=2 * rows * size * width, bytes_accessed=2 * size * width, transcendentals=0
        ),
    )(*blocks, perm, in_vmem(w))


def late_kernel(count, earlier, part, half, *refs):
    blocks, (perm, w), refs = refs[:count], refs[count : count + 2], refs[count + 2 :]
    totals, (keep, send, gathered) = refs[:earlier], refs[earlier:]
    x = gather_rows(blocks, perm, gathered)
    width = keep.shape[1]
    tile = tile_of(width)
    for n in range(0, width, tile):
        cols = slice(n, n + tile)
        there = slice(part * width + n, part * width + n + tile)
        product = jnp.dot(x, w[:, there], preferred_element_type=F32)
        for total in totals:
            product = product + total[:, there]
        keep[:, cols] = product[:half]
        send[:, cols] = product[half:]


def out_late(blocks, perm, w_last, totals, part, parts):
    rows = perm.shape[0]
    size, width = w_last.shape
    width //= parts
    out = jax.ShapeDtypeStruct((rows // 2, width), F32)
    return pl.pallas_call(
        functools.partial(late_kernel, len(blocks), len(totals), part, rows // 2),
        name=f"out_late_{part}",
        in_specs=[IN_VMEM] * (len(blocks) + 2 + len(totals)),
        out_specs=[IN_VMEM] * 2,
        out_shape=[out, out],
        scratch_shapes=[pltpu.VMEM((rows, size), BF16)],
        compiler_params=pltpu.CompilerParams(vmem_limit_bytes=6 * MIB),
        cost_estimate=pl.CostEstimate(
            flops=2 * rows * size * width, bytes_accessed=2 * size * width, transcendentals=0
        ),
    )(*blocks, perm, in_vmem(w_last), *[in_vmem(t) for t in totals])


def local(hidden, w_query, w_key, w_value, w_out, cache_keys, cache_values, lengths):
    nz, ny = lax.axis_size("gx"), lax.axis_size("gy")
    z, y = lax.axis_index("gx"), lax.axis_index("gy")
    rows_dev = lengths.shape[0]
    rows = rows_dev * nz * ny
    rows_y, rows_z = rows // ny, rows // nz
    chunks = w_key.shape[1] // HD
    chunk_cols = w_query.shape[1] // chunks
    depth = w_query.shape[0]
    high_first = list(reversed(bit_list(ny)))

    kz, ky, i = np.meshgrid(halves_order(nz), np.arange(ny), np.arange(rows_dev), indexing="ij")
    kz, ky, i = (jnp.asarray(a.reshape(-1), jnp.int32) for a in (kz, ky, i))
    row = ((kz ^ z) * ny + (ky ^ y)) * rows_dev + i
    perm_in = one_hot(((row // rows_y) ^ y) * rows_y + row % rows_y, rows)
    ko, t = np.meshgrid(halves_order(ny), np.arange(rows_y), indexing="ij")
    ko, t = (jnp.asarray(a.reshape(-1), jnp.int32) for a in (ko, t))
    row = (ko ^ y) * rows_y + t
    from_z, rest = row // rows_z, row % rows_z
    perm_out = one_hot(
        ((from_z ^ z) * ny + ((rest // rows_dev) ^ y)) * rows_dev + rest % rows_dev, rows
    )

    frequency = 500000.0 ** (-(jnp.arange(HD // 2, dtype=F32) * 2.0) / HD)
    angles = lengths.astype(F32)[:, None] * frequency[None, :]
    cosine, sine = jnp.cos(angles), jnp.sin(angles)
    cosine = jnp.tile(jnp.concatenate([cosine, cosine], axis=1), (ny, 1))
    sine = jnp.tile(jnp.concatenate([-sine, sine], axis=1), (ny, 1))

    query_cols = lambda c: pl.ds(c * chunk_cols, chunk_cols)
    all_depth, head = pl.ds(0, depth), pl.ds(0, HD)
    (w_first,) = fetch(
        "fetch_query",
        [after(w_query, z, y)],
        [(depth, chunk_cols)],
        [(0, (all_depth, query_cols(0)), 0, (all_depth, query_cols(0)))],
    )
    blocks = {0: hidden}
    far = high_first[0]
    for bit in high_first:
        blocks.update({k | bit: swap(b, "gy", bit) for k, b in list(blocks.items())})
        if bit == far:
            blocks[bit] = after(blocks[bit], w_first)
    w_kv = fetch(
        "fetch_key_value",
        [after(w_key, blocks[far]), w_value],
        [(depth, 2 * HD)] * chunks,
        [
            (n, (all_depth, pl.ds(c * HD, HD)), c, (all_depth, pl.ds(n * HD, HD)))
            for c in range(chunks)
            for n in range(2)
        ],
    )
    blocks = [blocks[k] for k in range(ny)]
    blocks[-1] = after(blocks[-1], *w_kv)

    keep, send, x, *early = project_first(blocks, perm_in, w_first, w_kv[0], w_query, chunks)
    projected = [(keep, send)]
    keys = values = None
    for c in range(1, chunks):
        last = c + 1 == chunks
        caches = (cache_keys, cache_values) if last else ()
        keep, send, *early = project_next(x, early[0], w_kv[c], w_query, c, chunks, caches)
        projected.append((keep, send))
        if last:
            keys, values = early

    def fetch_cache(sent):
        whole = tuple(pl.ds(0, n) for n in cache_keys.shape)
        return fetch(
            "fetch_cache",
            [after(cache_keys, sent), cache_values],
            [cache_keys.shape] * 2,
            [(n, whole, n, whole) for n in range(2)],
        )

    def fetch_out(c, sent):
        cols = pl.ds(0, w_out.shape[1])
        return fetch(
            f"fetch_out_{c}",
            [after(w_out, sent)],
            [(chunk_cols, w_out.shape[1])],
            [(0, (query_cols(c), cols), 0, (query_cols(0), cols))],
        )

    fetched, flying, sent = {}, {}, {}
    for bit in bit_list(nz):
        for c in range(chunks):
            if bit == 1:
                keep, send = projected[c]
            else:
                total = flying[c][0] + flying[c][1]
                middle = total.shape[0] // 2
                keep, send = total[:middle], total[middle:]
            flying[c] = (keep, swap(send, "gx", bit))
            sent[c] = send
    if keys is None:
        keys, values = fetch_cache(projected[-1][1])
    for c in range(chunks):
        other = chunks - 1 - c
        fetched[other] = fetch_out(other, sent[c])
        flying[c] = (flying[c][0], after(flying[c][1], *fetched[other]))

    totals = []
    attended = None
    for c in range(chunks):
        keep, arrived = flying[c]
        if attended is not None:
            arrived = after(arrived, attended)
        parts = {0: (keep + arrived).astype(BF16)}
        for bit in high_first:
            middle = parts[0].shape[0] // 2
            fresh = {}
            for k, part in parts.items():
                fresh[k] = part[:middle]
                fresh[k | bit] = swap(part[middle:], "gy", bit)
            parts = fresh
        groups = (jnp.arange(ny, dtype=jnp.int32) ^ y) * chunks + c
        keep, send = attend(
            [parts[k] for k in range(ny)], groups, lengths, cosine, sine, keys, values, c
        )
        attended = send
        parts = {0: keep, far: swap(send, "gy", far)}
        for bit in high_first[1:]:
            middle = parts[0].shape[0] // 2
            fresh = {}
            for k, part in parts.items():
                fresh[k] = part[:middle]
                fresh[k | bit] = swap(part[middle:], "gy", bit)
            parts = fresh
        mine = jnp.concatenate([parts[k] for k in range(ny)], axis=0)
        received = [mine] + [swap(mine, "gx", k) for k in range(1, nz)]
        if c + 1 < chunks:
            totals.append(out_early(received, perm_out, fetched[c][0], c))

    pieces = 2
    finished = []
    for part in range(pieces):
        keep, send = out_late(received, perm_out, fetched[chunks - 1][0], totals, part, pieces)
        for bit in bit_list(ny):
            if bit > 1:
                middle = total.shape[0] // 2
                keep, send = total[:middle], total[middle:]
            total = keep + swap(send, "gy", bit)
        finished.append(total.astype(BF16))
    return jnp.concatenate(finished, axis=1)


def solution(mesh):
    placed = (
        P(("groups", "gy"), "gx"),
        P("gx", "gy"),
        P("gx", "gy"),
        P("gx", "gy"),
        P("gy", "gx"),
        P(("groups", "gx", "gy"), None, None),
        P(("groups", "gx", "gy"), None, None),
        P(("groups", "gx", "gy")),
    )
    return jax.shard_map(
        local, mesh=mesh, in_specs=placed, out_specs=P(("groups", "gy"), "gx"), check_vma=False
    )
```

```python
import functools

import jax
import jax.numpy as jnp
import numpy as np
from jax import lax
from jax.experimental import pallas as pl
from jax.experimental.pallas import tpu as pltpu
from jax.sharding import PartitionSpec as P

HD = 128
MIB = 1 << 20
F32 = jnp.float32
BF16 = jnp.bfloat16


def swap(x, axis, offset):
    n = lax.axis_size(axis)
    return lax.ppermute(x, axis, [(i, i ^ offset) for i in range(n)])


def bit_list(n):
    return [1 << b for b in range(n.bit_length() - 1)]


def halves_order(n):
    bits = bit_list(n)
    out = []
    for position in range(n):
        k = 0
        for level, bit in enumerate(bits):
            if position >> (len(bits) - 1 - level) & 1:
                k |= bit
        out.append(k)
    return np.array(out)


def exchange(parts, bit):
    fresh = {}
    for k, part in parts.items():
        middle = part.shape[0] // 2
        fresh[k] = part[:middle]
        fresh[k | bit] = swap(part[middle:], "gy", bit)
    return fresh


def one_hot(columns, size):
    return (columns[:, None] == jnp.arange(size, dtype=jnp.int32)[None, :]).astype(BF16)


def in_hbm(x):
    return pltpu.with_memory_space_constraint(x, pltpu.HBM)


def in_vmem(x):
    return pltpu.with_memory_space_constraint(x, pltpu.VMEM)


ANYWHERE = pl.BlockSpec(memory_space=pl.ANY)
IN_VMEM = pl.BlockSpec(memory_space=pltpu.VMEM)
IN_SMEM = pl.BlockSpec(memory_space=pltpu.SMEM)


def row_pieces(rows, wanted=8):
    pieces = wanted
    while rows % pieces or (rows >= 16 * pieces and (rows // pieces) % 16):
        pieces //= 2
    return pieces


def copy_pieces(source, target, sems):
    pieces = row_pieces(target.shape[0])
    step = target.shape[0] // pieces

    def piece(n):
        at = pl.ds(pl.multiple_of(n * step, step), step)
        return pltpu.make_async_copy(source.at[at], target.at[at], sems.at[n])

    return pieces, piece


def start_copies(*copies):
    for pieces, piece in copies:
        pl.loop(0, pieces)(lambda n: piece(n).start())


def wait_copies(*copies):
    for pieces, piece in copies:
        pl.loop(0, pieces)(lambda n: piece(n).wait())


def fetch_kernel(plan, count, *refs):
    sources, targets, sems = refs[:count], refs[count:-1], refs[-1]
    copies = [
        copy_pieces(sources[source].at[window], targets[target].at[place], sems.at[n])
        for n, (source, window, target, place) in enumerate(plan)
    ]
    start_copies(*copies)
    wait_copies(*copies)


def fetch(name, arrays, shapes, plan):
    return pl.pallas_call(
        functools.partial(fetch_kernel, plan, len(arrays)),
        name=name,
        in_specs=[ANYWHERE] * len(arrays),
        out_specs=[IN_VMEM] * len(shapes),
        out_shape=[pltpu.VMEM(shape, BF16) for shape in shapes],
        scratch_shapes=[pltpu.SemaphoreType.DMA((len(plan), 8))],
        compiler_params=pltpu.CompilerParams(vmem_limit_bytes=MIB),
        cost_estimate=pl.CostEstimate(
            flops=0, bytes_accessed=2 * sum(int(np.prod(shape)) for shape in shapes), transcendentals=0
        ),
    )(*[in_hbm(a) for a in arrays])


def after(x, *done):
    return lax.optimization_barrier((x, *done))[0]


def tile_of(width, wanted=512):
    return wanted if width % wanted == 0 else width


FINE, COARSE = 8372224.0, 32752.0


def coded_width(cols, fine):
    return cols + (cols // 2 if fine else 0) + HD


def encode(coded, value, cols, fine):
    lane = lax.broadcasted_iota(jnp.int32, (coded.shape[0], HD), 1)
    exponents = jnp.zeros(lane.shape, jnp.int32)
    lower = None
    for g in range(cols // HD):
        v = value(slice(g * HD, (g + 1) * HD))
        largest = jnp.max(jnp.abs(v), axis=1, keepdims=True)
        exponent = jnp.maximum(jnp.ceil(jnp.log2(jnp.maximum(largest, 1e-31))), -100.0)
        n = jnp.floor(v * ((FINE if fine else COARSE) / jnp.exp2(exponent)) + 0.5).astype(jnp.int32)
        exponents = jnp.where(lane == g, exponent.astype(jnp.int32), exponents)
        if fine:
            coded[:, g * HD : (g + 1) * HD] = (n >> 8).astype(jnp.int16)
            if g % 2 == 0:
                lower = n & 255
            else:
                both = lower * 256 + (n & 255) - 32768
                coded[:, cols + g // 2 * HD : cols + (g // 2 + 1) * HD] = both.astype(jnp.int16)
        else:
            coded[:, g * HD : (g + 1) * HD] = n.astype(jnp.int16)
    coded[:, coded.shape[1] - HD :] = exponents.astype(jnp.int16)


def decode(coded, cols, fine):
    scales = jnp.exp2(coded[:, coded.shape[1] - HD :].astype(F32)) / (FINE if fine else COARSE)
    for g in range(cols // HD):
        n = coded[:, g * HD : (g + 1) * HD].astype(jnp.int32)
        if fine:
            if g % 2 == 0:
                both = coded[:, cols + g // 2 * HD : cols + (g // 2 + 1) * HD].astype(jnp.int32) + 32768
            n = n * 256 + ((both >> 8) if g % 2 == 0 else (both & 255))
        yield slice(g * HD, (g + 1) * HD), n.astype(F32) * scales[:, g : g + 1]


def pass_kernel(fine, coded_in, keep, *refs):
    if coded_in.dtype == jnp.int16:
        arrived = decode(coded_in, keep.shape[1], fine)
    else:
        arrived = ((slice(g, g + HD), coded_in[:, g : g + HD]) for g in range(0, keep.shape[1], HD))
    kept, coded_out, total = refs
    half = kept.shape[0]
    for cols, value in arrived:
        value = keep[:, cols] + value
        kept[:, cols] = value[:half]
        total[:, cols] = value[half:]
    encode(coded_out, lambda cols: total[:, cols], keep.shape[1], fine)


def pass_on(name, arrived, keep, fine):
    rows, cols = keep.shape[0] // 2, keep.shape[1]
    return pl.pallas_call(
        functools.partial(pass_kernel, fine),
        name=name,
        in_specs=[IN_VMEM] * 2,
        out_specs=[IN_VMEM] * 2,
        out_shape=[
            jax.ShapeDtypeStruct((rows, cols), F32),
            jax.ShapeDtypeStruct((rows, coded_width(cols, fine)), jnp.int16),
        ],
        scratch_shapes=[pltpu.VMEM((rows, cols), F32)],
        compiler_params=pltpu.CompilerParams(vmem_limit_bytes=6 * MIB),
        cost_estimate=pl.CostEstimate(flops=40 * rows * cols, bytes_accessed=16 * rows * cols, transcendentals=0),
    )(arrived, keep)


def finish_rows_kernel(coded, keep, *halves):
    rows = halves[0].shape[0]
    for cols, value in decode(coded, keep.shape[1], True):
        value = keep[:, cols] + value
        for n, half in enumerate(halves):
            half[:, cols] = value[n * rows : (n + 1) * rows].astype(BF16)


def finish_rows(name, arrived, keep):
    rows, cols = keep.shape[0] // 2, keep.shape[1]
    return pl.pallas_call(
        finish_rows_kernel,
        name=name,
        in_specs=[IN_VMEM] * 2,
        out_specs=[IN_VMEM] * 2,
        out_shape=[jax.ShapeDtypeStruct((rows, cols), BF16)] * 2,
        compiler_params=pltpu.CompilerParams(vmem_limit_bytes=6 * MIB),
        cost_estimate=pl.CostEstimate(flops=20 * rows * cols, bytes_accessed=16 * rows * cols, transcendentals=0),
    )(arrived, keep)


def finish_out_kernel(count, *refs):
    coded, keeps, out = refs[:count], refs[count : 2 * count], refs[2 * count]
    at = 0
    for arrived, keep in zip(coded, keeps):
        width = keep.shape[1]
        for cols, value in decode(arrived, width, False):
            out[:, at + cols.start : at + cols.stop] = (keep[:, cols] + value).astype(BF16)
        at += width


def finish_out(arrived, keeps):
    rows, cols = keeps[0].shape[0], sum(k.shape[1] for k in keeps)
    return pl.pallas_call(
        functools.partial(finish_out_kernel, len(keeps)),
        name="finish_out",
        in_specs=[IN_VMEM] * (2 * len(keeps)),
        out_specs=IN_VMEM,
        out_shape=jax.ShapeDtypeStruct((rows, cols), BF16),
        compiler_params=pltpu.CompilerParams(vmem_limit_bytes=8 * MIB),
        cost_estimate=pl.CostEstimate(flops=20 * rows * cols, bytes_accessed=16 * rows * cols, transcendentals=0),
    )(*arrived, *keeps)


def put(keep, send, cols, product, more):
    half = keep.shape[0]
    if more:
        keep[:, cols] += product[:half]
        send[:, cols] += product[half:]
    else:
        keep[:, cols] = product[:half]
        send[:, cols] = product[half:]


def multiply(x, weights, keep, send, more):
    tile = tile_of(weights.shape[1])
    for n in range(0, weights.shape[1], tile):
        product = jnp.dot(x, weights[:, n : n + tile], preferred_element_type=F32)
        put(keep, send, slice(n, n + tile), product, more)


def first_kernel(count, held, chunks, quarter, *refs):
    blocks, refs = refs[:count], refs[count:]
    perm, refs = refs[0], refs[1:]
    early, (wq, wk, wv), refs = refs[:held], refs[held : held + 3], refs[held + 3 :]
    keep, coded, x = refs[:3]
    others, refs = refs[3 : 2 + chunks], refs[2 + chunks :]
    send, late, wk_here, wv_here, gathered, sems = refs
    pieces, _, qc = late.shape
    copies = [
        copy_pieces(wq.at[pl.ds((held + n) * quarter, quarter), pl.ds(0, qc)], late.at[n], sems.at[n])
        for n in range(pieces)
    ]
    copies += [copy_pieces(wk, wk_here, sems.at[pieces]), copy_pieces(wv, wv_here, sems.at[pieces + 1])]
    start_copies(*copies[:2])
    rows = blocks[0].shape[0]
    for k in range(count):
        gathered[k * rows : (k + 1) * rows, :] = blocks[k][...]
    width = x.shape[1]
    tile = tile_of(width)
    for at in range(0, width, tile):
        x[:, at : at + tile] = jnp.dot(
            perm[...], gathered[:, at : at + tile], preferred_element_type=F32
        ).astype(BF16)
    for n, w in enumerate(early):
        multiply(x[:, n * quarter : (n + 1) * quarter], w, keep, send, n > 0)
    for n in range(pieces):
        wait_copies(copies[n])
        start_copies(*copies[n + 2 : n + 3])
        at = (held + n) * quarter
        multiply(x[:, at : at + quarter], late.at[n], keep, send, held + n > 0)
    for n, w in enumerate((wk_here, wv_here)):
        wait_copies(copies[pieces + n])
        product = jnp.dot(x[...], w[...], preferred_element_type=F32)
        put(keep, send, slice(qc + n * HD, qc + (n + 1) * HD), product[:, :HD], False)
        for c, other in enumerate(others):
            other[:, n * HD : (n + 1) * HD] = product[:, (c + 1) * HD : (c + 2) * HD]
    encode(coded, lambda cols: send[:, cols], keep.shape[1], True)


def project_first(blocks, perm, early, w_query, w_key, w_value, chunks):
    rows = perm.shape[0]
    depth = w_query.shape[0]
    quarter = depth // 4
    qc, kc = w_query.shape[1] // chunks, w_key.shape[1]
    width = qc + 2 * HD
    held = len(early)
    pieces = 4 - held
    out = jax.ShapeDtypeStruct((rows // 2, width), F32)
    coded = jax.ShapeDtypeStruct((rows // 2, coded_width(width, True)), jnp.int16)
    return pl.pallas_call(
        functools.partial(first_kernel, len(blocks), held, chunks, quarter),
        name="project_first",
        in_specs=[IN_VMEM] * (len(blocks) + 1 + held) + [ANYWHERE] * 3,
        out_specs=[IN_VMEM] * (2 + chunks),
        out_shape=[out, coded, pltpu.VMEM((rows, depth), BF16)]
        + [jax.ShapeDtypeStruct((rows, 2 * HD), F32)] * (chunks - 1),
        scratch_shapes=[
            pltpu.VMEM((rows // 2, width), F32),
            pltpu.VMEM((pieces, quarter, qc), BF16),
            pltpu.VMEM((depth, kc), BF16),
            pltpu.VMEM((depth, kc), BF16),
            pltpu.VMEM((rows, depth), BF16),
            pltpu.SemaphoreType.DMA((pieces + 2, 8)),
        ],
        compiler_params=pltpu.CompilerParams(vmem_limit_bytes=18 * MIB),
        cost_estimate=pl.CostEstimate(
            flops=2 * rows * depth * width, bytes_accessed=4 * depth * width, transcendentals=0
        ),
    )(*blocks, perm, *[in_vmem(w) for w in early], in_hbm(w_query), in_hbm(w_key), in_hbm(w_value))


def next_kernel(chunk, quarter, x, kv, wq, *refs):
    keep, coded, send, late, sems = refs
    pieces, _, qc = late.shape
    copies = [
        copy_pieces(wq.at[pl.ds(n * quarter, quarter), pl.ds(chunk * qc, qc)], late.at[n], sems.at[n])
        for n in range(pieces)
    ]
    start_copies(*copies[:2])
    put(keep, send, slice(qc, qc + 2 * HD), kv[...], False)
    for n in range(pieces):
        wait_copies(copies[n])
        start_copies(*copies[n + 2 : n + 3])
        multiply(x[:, n * quarter : (n + 1) * quarter], late.at[n], keep, send, n > 0)
    encode(coded, lambda cols: send[:, cols], keep.shape[1], True)


def project_next(x, kv, w_query, chunk, chunks):
    rows, depth = x.shape
    quarter, qc = depth // 4, w_query.shape[1] // chunks
    width = qc + 2 * HD
    out = jax.ShapeDtypeStruct((rows // 2, width), F32)
    coded = jax.ShapeDtypeStruct((rows // 2, coded_width(width, True)), jnp.int16)
    return pl.pallas_call(
        functools.partial(next_kernel, chunk, quarter),
        name=f"project_next_{chunk}",
        in_specs=[IN_VMEM] * 2 + [ANYWHERE],
        out_specs=[IN_VMEM] * 2,
        out_shape=[out, coded],
        scratch_shapes=[
            pltpu.VMEM((rows // 2, width), F32),
            pltpu.VMEM((4, quarter, qc), BF16),
            pltpu.SemaphoreType.DMA((4, 8)),
        ],
        compiler_params=pltpu.CompilerParams(vmem_limit_bytes=20 * MIB),
        cost_estimate=pl.CostEstimate(
            flops=2 * rows * depth * width, bytes_accessed=4 * depth * width, transcendentals=0
        ),
    )(x, kv, in_hbm(w_query))


def attend_kernel(count, heads, joined, groups, lengths, *refs):
    blocks, (cosine, sine, keys, values), refs = refs[:count], refs[count : count + 4], refs[count + 4 :]
    before, (keep, send), refs = refs[:joined], refs[joined : joined + 2], refs[joined + 2 :]
    packed, staged, scores, weights_low, mixed = refs
    rows = blocks[0].shape[0]
    pairs = count * rows
    slots = keys.shape[1]
    query_cols = heads * HD
    scale = 1.0 / jnp.sqrt(jnp.float32(HD))
    cos, sin = cosine[...], sine[...]

    def rotated(u):
        return u * cos + pltpu.roll(u, HD // 2, 1) * sin

    for k in range(count):
        packed[k * rows : (k + 1) * rows, :] = blocks[k][...].astype(F32)
    for h in range(heads):
        staged[:, h, :] = rotated(packed[:, h * HD : (h + 1) * HD])
    key_rot = rotated(packed[:, query_cols : query_cols + HD]).astype(BF16).astype(F32)
    slot = lax.broadcasted_iota(jnp.int32, (heads, slots), 1)

    def lanes(k):
        return pl.ds(pl.multiple_of(groups[k] * HD, HD), HD)

    for p in range(pairs):
        k, r = divmod(p, rows)
        scores[p] = lax.dot_general(
            staged[p].astype(BF16), keys[r, :, lanes(k)], (((1,), (1,)), ((), ())), preferred_element_type=F32
        )
    owns, denominators = [], []
    for p in range(pairs):
        r = p % rows
        q = staged[p].astype(BF16).astype(F32)
        masked = jnp.where(slot < lengths[r], scores[p] * scale, -jnp.inf)
        own = jnp.sum(q * key_rot[p : p + 1], axis=1, keepdims=True) * scale
        highest = jnp.maximum(jnp.max(masked, axis=1, keepdims=True), own)
        weights = jnp.exp(masked - highest)
        own_weight = jnp.exp(own - highest)
        denominators.append(jnp.sum(weights, axis=1, keepdims=True) + own_weight)
        owns.append(own_weight.astype(BF16).astype(F32))
        weights_low[p] = weights.astype(BF16)
    for p in range(pairs):
        k, r = divmod(p, rows)
        mixture = jnp.dot(weights_low[p], values[r, :, lanes(k)], preferred_element_type=F32)
        mixture = mixture + owns[p] * packed[p : p + 1, query_cols + HD :]
        mixed[p] = mixture / denominators[p]
    half = pairs // 2
    at = 0
    if joined:
        at = before[0].shape[1]
        keep[:, :at] = before[0][...]
        send[:, :at] = before[1][...]
    for h in range(heads):
        low = mixed[:, h, :].astype(BF16)
        keep[:, at + h * HD : at + (h + 1) * HD] = low[:half]
        send[:, at + h * HD : at + (h + 1) * HD] = low[half:]


def attend(blocks, groups, lengths, cosine, sine, cache_keys, cache_values, before):
    rows, width = blocks[0].shape
    heads = (width - 2 * HD) // HD
    count = len(blocks)
    pairs = count * rows
    slots = cache_keys.shape[1]
    done = before[0].shape[1] if before else 0
    out = jax.ShapeDtypeStruct((pairs // 2, done + heads * HD), BF16)
    return pl.pallas_call(
        functools.partial(attend_kernel, count, heads, len(before)),
        name=f"attend_{done // (heads * HD)}",
        in_specs=[IN_SMEM, IN_SMEM] + [IN_VMEM] * (count + 4 + len(before)),
        out_specs=[IN_VMEM] * 2,
        out_shape=[out, out],
        scratch_shapes=[
            pltpu.VMEM((pairs, width), F32),
            pltpu.VMEM((pairs, heads, HD), F32),
            pltpu.VMEM((pairs, heads, slots), F32),
            pltpu.VMEM((pairs, heads, slots), BF16),
            pltpu.VMEM((pairs, heads, HD), F32),
        ],
        compiler_params=pltpu.CompilerParams(vmem_limit_bytes=8 * MIB),
        cost_estimate=pl.CostEstimate(
            flops=4 * pairs * heads * HD * slots, bytes_accessed=4 * rows * slots * count * HD, transcendentals=0
        ),
    )(groups, lengths, *blocks, cosine, sine, in_vmem(cache_keys), in_vmem(cache_values), *before)


def out_kernel(count, held, part, fresh, *refs):
    blocks, refs = refs[:count], refs[count:]
    weights, refs = refs[:held], refs[held:]
    if fresh:
        perm, keep, send, x, gathered = refs
        rows = blocks[0].shape[0]
        for k, block in enumerate(blocks):
            gathered[k * rows : (k + 1) * rows, :] = block[...]
        tile = tile_of(x.shape[1])
        for at in range(0, x.shape[1], tile):
            x[:, at : at + tile] = jnp.dot(
                perm[...], gathered[:, at : at + tile], preferred_element_type=F32
            ).astype(BF16)
    else:
        (x,), (keep, send) = blocks, refs
    half, width = keep.shape
    tile = tile_of(width)
    for n in range(0, width, tile):
        cols = slice(n, n + tile)
        there = slice(part * width + n, part * width + n + tile)
        at, product = 0, None
        for w in weights:
            term = jnp.dot(x[:, at : at + w.shape[0]], w[:, there], preferred_element_type=F32)
            product = term if product is None else product + term
            at += w.shape[0]
        keep[:, cols] = product[:half]
        send[:, cols] = product[half:]


def out_project(blocks, weights, part, parts, perm=None):
    fresh = perm is not None
    size = blocks[0].shape[1]
    rows = sum(b.shape[0] for b in blocks)
    width = weights[0].shape[1] // parts
    out = jax.ShapeDtypeStruct((rows // 2, width), F32)
    return pl.pallas_call(
        functools.partial(out_kernel, len(blocks), len(weights), part, fresh),
        name=f"out_project_{part}",
        in_specs=[IN_VMEM] * (len(blocks) + len(weights) + fresh),
        out_specs=[IN_VMEM] * (2 + fresh),
        out_shape=[out, out] + [pltpu.VMEM((rows, size), BF16)] * fresh,
        scratch_shapes=[pltpu.VMEM((rows, size), BF16)] * fresh,
        compiler_params=pltpu.CompilerParams(vmem_limit_bytes=6 * MIB),
        cost_estimate=pl.CostEstimate(
            flops=2 * rows * size * width, bytes_accessed=2 * size * width, transcendentals=0
        ),
    )(*blocks, *[in_vmem(w) for w in weights], *([perm] if fresh else []))


def local(hidden, w_query, w_key, w_value, w_out, cache_keys, cache_values, lengths):
    nz, ny = lax.axis_size("gx"), lax.axis_size("gy")
    z, y = lax.axis_index("gx"), lax.axis_index("gy")
    rows_dev = lengths.shape[0]
    rows = rows_dev * nz * ny
    rows_y, rows_z = rows // ny, rows // nz
    chunks = w_key.shape[1] // HD
    chunk_cols = w_query.shape[1] // chunks
    depth = w_query.shape[0]
    high_first = list(reversed(bit_list(ny)))

    kz, ky, i = np.meshgrid(halves_order(nz), np.arange(ny), np.arange(rows_dev), indexing="ij")
    kz, ky, i = (jnp.asarray(a.reshape(-1), jnp.int32) for a in (kz, ky, i))
    row = ((kz ^ z) * ny + (ky ^ y)) * rows_dev + i
    perm_in = one_hot(((row // rows_y) ^ y) * rows_y + row % rows_y, rows)
    ko, t = np.meshgrid(halves_order(ny), np.arange(rows_y), indexing="ij")
    ko, t = (jnp.asarray(a.reshape(-1), jnp.int32) for a in (ko, t))
    row = (ko ^ y) * rows_y + t
    from_z, rest = row // rows_z, row % rows_z
    perm_out = one_hot(
        ((from_z ^ z) * ny + ((rest // rows_dev) ^ y)) * rows_dev + rest % rows_dev, rows
    )

    frequency = 500000.0 ** (-(jnp.arange(HD // 2, dtype=F32) * 2.0) / HD)
    angles = lengths.astype(F32)[:, None] * frequency[None, :]
    cosine, sine = jnp.cos(angles), jnp.sin(angles)
    cosine = jnp.tile(jnp.concatenate([cosine, cosine], axis=1), (ny, 1))
    sine = jnp.tile(jnp.concatenate([-sine, sine], axis=1), (ny, 1))

    quarter = depth // 4
    cols = pl.ds(0, chunk_cols)

    def fetch_query(first, last, *done):
        shape = (quarter, chunk_cols)
        return fetch(
            f"fetch_query_{first}",
            [after(w_query, *done)],
            [shape] * (last - first),
            [
                (0, (pl.ds((first + n) * quarter, quarter), cols), n, (pl.ds(0, quarter), cols))
                for n in range(last - first)
            ],
        )

    blocks = {0: hidden}
    far = high_first[0]
    early = fetch_query(0, 2, z, y)
    for bit in high_first:
        blocks.update({k | bit: swap(b, "gy", bit) for k, b in list(blocks.items())})
        if bit == far:
            blocks[bit] = after(blocks[bit], *early)
    blocks = [blocks[k] for k in range(ny)]

    keep, send, x, *rest = project_first(blocks, perm_in, early, w_query, w_key, w_value, chunks)
    projected = [(keep, send)]
    for c in range(1, chunks):
        projected.append(project_next(x, rest[c - 1], w_query, c, chunks))

    sixteenth = w_out.shape[0] // 16

    def fetch_out(first, last, sent, others=()):
        shapes = [((last - first) * sixteenth, w_out.shape[1])] + [a.shape for a in others]
        window = (pl.ds(first * sixteenth, shapes[0][0]), pl.ds(0, shapes[0][1]))
        plan = [(0, window, 0, tuple(pl.ds(0, n) for n in shapes[0]))]
        for n, a in enumerate(others):
            whole = tuple(pl.ds(0, d) for d in a.shape)
            plan.append((n + 1, whole, n + 1, whole))
        return fetch(f"fetch_{first}_{last}", [after(w_out, sent), *others], shapes, plan)

    flying, sent = {}, {}
    for bit in bit_list(nz):
        for c in range(chunks):
            if bit == 1:
                keep, send = projected[c]
            else:
                keep, send = pass_on(f"pass_on_{c}_{bit}", flying[c][1], flying[c][0], True)
            flying[c] = (keep, swap(send, "gx", bit))
            sent[c] = send
            if bit == 2 and c == 0:
                w_0, keys, values = fetch_out(0, 4, send, (cache_keys, cache_values))
                last = chunks - 1
                flying[last] = (flying[last][0], after(flying[last][1], w_0, keys, values))

    heads_of = []
    for c in range(chunks):
        keep, arrived = flying[c]
        if c == 1:
            arrived = after(arrived, w_1)
        keep, send = finish_rows(f"finish_rows_{c}", arrived, keep)
        arrived = swap(send, "gy", far)
        if c == 0:
            (w_1,) = fetch_out(4, 7, send)
            arrived = after(arrived, w_1)
        heads_of.append((keep, send, arrived))
    before = ()
    for c, (keep, _, arrived) in enumerate(heads_of):
        if before:
            arrived = after(arrived, before[1])
        parts = {0: keep, far: arrived}
        for bit in high_first[1:]:
            parts = exchange(parts, bit)
        if c + 1 < chunks:
            parts[ny - 1] = after(parts[ny - 1], heads_of[c + 1][1])
        groups = (jnp.arange(ny, dtype=jnp.int32) ^ y) * chunks + c
        before = attend(
            [parts[k] for k in range(ny)], groups, lengths, cosine, sine, keys, values, before
        )
    (w_2,) = fetch_out(7, 10, before[1])
    parts = {0: before[0], far: after(swap(before[1], "gy", far), w_2)}
    for bit in high_first[1:]:
        parts = exchange(parts, bit)
    mine = jnp.concatenate([parts[k] for k in range(ny)], axis=0)
    (w_3,) = fetch_out(10, 16, mine)
    received = [mine] + [swap(mine, "gx", k) for k in range(1, nz)]
    received[-1] = after(received[-1], w_3)
    weights = [w_0, w_1, w_2, w_3]

    pieces = 2
    arrived, keeps = [], []
    for part in range(pieces):
        if part == 0:
            keep, send, x = out_project(received, weights, part, pieces, perm_out)
        else:
            keep, send = out_project([x], weights, part, pieces)
        for bit in bit_list(ny)[1:]:
            keep, send = pass_on(f"out_pass_{part}_{bit}", swap(send, "gy", bit // 2), keep, False)
        keeps.append(keep)
        arrived.append(swap(send, "gy", far))
    return finish_out(arrived, keeps)


def solution(mesh):
    placed = (
        P(("groups", "gy"), "gx"),
        P("gx", "gy"),
        P("gx", "gy"),
        P("gx", "gy"),
        P("gy", "gx"),
        P(("groups", "gx", "gy"), None, None),
        P(("groups", "gx", "gy"), None, None),
        P(("groups", "gx", "gy")),
    )
    return jax.shard_map(
        local, mesh=mesh, in_specs=placed, out_specs=P(("groups", "gy"), "gx"), check_vma=False
    )
```

```python
import functools

import jax
import jax.numpy as jnp
import numpy as np
from jax import lax
from jax.experimental import pallas as pl
from jax.experimental.pallas import tpu as pltpu
from jax.sharding import PartitionSpec as P

HD = 128
MIB = 1 << 20
F32 = jnp.float32
BF16 = jnp.bfloat16


def swap(x, axis, offset):
    n = lax.axis_size(axis)
    return lax.ppermute(x, axis, [(i, i ^ offset) for i in range(n)])


def bit_list(n):
    return [1 << b for b in range(n.bit_length() - 1)]


def halves_order(n):
    bits = bit_list(n)
    out = []
    for position in range(n):
        k = 0
        for level, bit in enumerate(bits):
            if position >> (len(bits) - 1 - level) & 1:
                k |= bit
        out.append(k)
    return np.array(out)


def exchange(parts):
    return [parts[0]] + [swap(parts[k], "gy", k) for k in range(1, len(parts))]


def one_hot(columns, size):
    return (columns[:, None] == jnp.arange(size, dtype=jnp.int32)[None, :]).astype(BF16)


def in_hbm(x):
    return pltpu.with_memory_space_constraint(x, pltpu.HBM)


def in_vmem(x):
    return pltpu.with_memory_space_constraint(x, pltpu.VMEM)


ANYWHERE = pl.BlockSpec(memory_space=pl.ANY)
IN_VMEM = pl.BlockSpec(memory_space=pltpu.VMEM)
IN_SMEM = pl.BlockSpec(memory_space=pltpu.SMEM)


def row_pieces(rows, wanted):
    pieces = wanted
    while rows % pieces or (rows >= 16 * pieces and (rows // pieces) % 16):
        pieces //= 2
    return pieces


def copy_pieces(source, target, sems, wanted=8):
    pieces = row_pieces(target.shape[0], wanted)
    step = target.shape[0] // pieces

    def piece(n):
        at = pl.ds(pl.multiple_of(n * step, step), step)
        return pltpu.make_async_copy(source.at[at], target.at[at], sems.at[n])

    return pieces, piece


def start_copies(*copies):
    for pieces, piece in copies:
        pl.loop(0, pieces)(lambda n: piece(n).start())


def wait_copies(*copies):
    for pieces, piece in copies:
        pl.loop(0, pieces)(lambda n: piece(n).wait())


def fetch_kernel(plan, count, *refs):
    sources, targets, sems = refs[:count], refs[count:-1], refs[-1]
    copies = [
        copy_pieces(sources[source].at[window], targets[target].at[place], sems.at[n])
        for n, (source, window, target, place) in enumerate(plan)
    ]
    start_copies(*copies)
    wait_copies(*copies)


def fetch(name, arrays, shapes, plan):
    return pl.pallas_call(
        functools.partial(fetch_kernel, plan, len(arrays)),
        name=name,
        in_specs=[ANYWHERE] * len(arrays),
        out_specs=[IN_VMEM] * len(shapes),
        out_shape=[pltpu.VMEM(shape, BF16) for shape in shapes],
        scratch_shapes=[pltpu.SemaphoreType.DMA((len(plan), 8))],
        compiler_params=pltpu.CompilerParams(vmem_limit_bytes=MIB),
        cost_estimate=pl.CostEstimate(
            flops=0, bytes_accessed=2 * sum(int(np.prod(shape)) for shape in shapes), transcendentals=0
        ),
    )(*[in_hbm(a) for a in arrays])


def after(x, *done):
    return lax.optimization_barrier((x, *done))[0]


def tile_of(width, wanted=512):
    return wanted if width % wanted == 0 else width


FINE, COARSE = 8372224.0, 32752.0


def coded_width(cols, fine):
    return cols + (cols // 2 if fine else 0) + HD


def encode(coded, value, cols, fine):
    lane = lax.broadcasted_iota(jnp.int32, (coded.shape[0], HD), 1)
    exponents = jnp.zeros(lane.shape, jnp.int32)
    lower = None
    for g in range(cols // HD):
        v = value(slice(g * HD, (g + 1) * HD))
        largest = jnp.max(jnp.abs(v), axis=1, keepdims=True)
        exponent = jnp.maximum(jnp.ceil(jnp.log2(jnp.maximum(largest, 1e-31))), -100.0)
        n = jnp.floor(v * ((FINE if fine else COARSE) / jnp.exp2(exponent)) + 0.5).astype(jnp.int32)
        exponents = jnp.where(lane == g, exponent.astype(jnp.int32), exponents)
        if fine:
            coded[:, g * HD : (g + 1) * HD] = (n >> 8).astype(jnp.int16)
            if g % 2 == 0:
                lower = n & 255
            else:
                both = lower * 256 + (n & 255) - 32768
                coded[:, cols + g // 2 * HD : cols + (g // 2 + 1) * HD] = both.astype(jnp.int16)
        else:
            coded[:, g * HD : (g + 1) * HD] = n.astype(jnp.int16)
    coded[:, coded.shape[1] - HD :] = exponents.astype(jnp.int16)


def decode(coded, cols, fine):
    scales = jnp.exp2(coded[:, coded.shape[1] - HD :].astype(F32)) / (FINE if fine else COARSE)
    for g in range(cols // HD):
        n = coded[:, g * HD : (g + 1) * HD].astype(jnp.int32)
        if fine:
            if g % 2 == 0:
                both = coded[:, cols + g // 2 * HD : cols + (g // 2 + 1) * HD].astype(jnp.int32) + 32768
            n = n * 256 + ((both >> 8) if g % 2 == 0 else (both & 255))
        yield slice(g * HD, (g + 1) * HD), n.astype(F32) * scales[:, g : g + 1]


def pass_kernel(fine, coded_in, keep, *refs):
    if coded_in.dtype == jnp.int16:
        arrived = decode(coded_in, keep.shape[1], fine)
    else:
        arrived = ((slice(g, g + HD), coded_in[:, g : g + HD]) for g in range(0, keep.shape[1], HD))
    kept, coded_out, total = refs
    half = kept.shape[0]
    for cols, value in arrived:
        value = keep[:, cols] + value
        kept[:, cols] = value[:half]
        total[:, cols] = value[half:]
    encode(coded_out, lambda cols: total[:, cols], keep.shape[1], fine)


def pass_on(name, arrived, keep, fine):
    rows, cols = keep.shape[0] // 2, keep.shape[1]
    return pl.pallas_call(
        functools.partial(pass_kernel, fine),
        name=name,
        in_specs=[IN_VMEM] * 2,
        out_specs=[IN_VMEM] * 2,
        out_shape=[
            jax.ShapeDtypeStruct((rows, cols), F32),
            jax.ShapeDtypeStruct((rows, coded_width(cols, fine)), jnp.int16),
        ],
        scratch_shapes=[pltpu.VMEM((rows, cols), F32)],
        compiler_params=pltpu.CompilerParams(vmem_limit_bytes=6 * MIB),
        cost_estimate=pl.CostEstimate(flops=40 * rows * cols, bytes_accessed=16 * rows * cols, transcendentals=0),
    )(arrived, keep)


def finish_rows_kernel(coded, keep, *parts):
    rows = parts[0].shape[0]
    for cols, value in decode(coded, keep.shape[1], True):
        value = keep[:, cols] + value
        for n, part in enumerate(parts):
            part[:, cols] = value[n * rows : (n + 1) * rows].astype(BF16)


def finish_rows(name, arrived, keep, parts):
    rows, cols = keep.shape[0] // parts, keep.shape[1]
    return pl.pallas_call(
        finish_rows_kernel,
        name=name,
        in_specs=[IN_VMEM] * 2,
        out_specs=[IN_VMEM] * parts,
        out_shape=[jax.ShapeDtypeStruct((rows, cols), BF16)] * parts,
        compiler_params=pltpu.CompilerParams(vmem_limit_bytes=6 * MIB),
        cost_estimate=pl.CostEstimate(flops=20 * rows * cols, bytes_accessed=16 * rows * cols, transcendentals=0),
    )(arrived, keep)


def finish_out_kernel(count, *refs):
    coded, keeps, out = refs[:count], refs[count : 2 * count], refs[2 * count]
    at = 0
    for arrived, keep in zip(coded, keeps):
        width = keep.shape[1]
        for cols, value in decode(arrived, width, False):
            out[:, at + cols.start : at + cols.stop] = (keep[:, cols] + value).astype(BF16)
        at += width


def finish_out(arrived, keeps):
    rows, cols = keeps[0].shape[0], sum(k.shape[1] for k in keeps)
    return pl.pallas_call(
        functools.partial(finish_out_kernel, len(keeps)),
        name="finish_out",
        in_specs=[IN_VMEM] * (2 * len(keeps)),
        out_specs=IN_VMEM,
        out_shape=jax.ShapeDtypeStruct((rows, cols), BF16),
        compiler_params=pltpu.CompilerParams(vmem_limit_bytes=8 * MIB),
        cost_estimate=pl.CostEstimate(flops=20 * rows * cols, bytes_accessed=16 * rows * cols, transcendentals=0),
    )(*arrived, *keeps)


def put(keep, send, cols, product, more):
    half = keep.shape[0]
    if more:
        keep[:, cols] += product[:half]
        send[:, cols] += product[half:]
    else:
        keep[:, cols] = product[:half]
        send[:, cols] = product[half:]


def multiply(x, weights, keep, send, more):
    tile = tile_of(weights.shape[1])
    for n in range(0, weights.shape[1], tile):
        product = jnp.dot(x, weights[:, n : n + tile], preferred_element_type=F32)
        put(keep, send, slice(n, n + tile), product, more)


def first_kernel(count, chunks, *refs):
    blocks, refs = refs[:count], refs[count:]
    perm, early, wk, wq, wv, keep, coded, x = refs[:8]
    others, refs = refs[8 : 7 + chunks], refs[7 + chunks :]
    ahead, refs = (refs[:1], refs[1:]) if chunks > 1 else ((), refs)
    send, late, wv_here, gathered, sems = refs
    held = early.shape[0]
    pieces, depth, qc = late.shape
    copies = [
        copy_pieces(wq.at[pl.ds(held + n * depth, depth), pl.ds(0, qc)], late.at[n], sems.at[n], 2)
        for n in range(pieces)
    ]
    copies.append(copy_pieces(wv, wv_here, sems.at[pieces], 4))
    for w in ahead:
        copies.append(copy_pieces(wq.at[pl.ds(0, w.shape[0]), pl.ds(qc, qc)], w, sems.at[pieces + 1], 4))
    start_copies(*copies)
    rows = blocks[0].shape[0]
    for k in range(count):
        gathered[k * rows : (k + 1) * rows, :] = blocks[k][...]
    width = x.shape[1]
    tile = tile_of(width)
    for at in range(0, width, tile):
        x[:, at : at + tile] = jnp.dot(
            perm[...], gathered[:, at : at + tile], preferred_element_type=F32
        ).astype(BF16)
    multiply(x[:, :held], early, keep, send, False)

    def key_or_value(n, w):
        product = jnp.dot(x[...], w[...], preferred_element_type=F32)
        put(keep, send, slice(qc + n * HD, qc + (n + 1) * HD), product[:, :HD], False)
        for c, other in enumerate(others):
            other[:, n * HD : (n + 1) * HD] = product[:, (c + 1) * HD : (c + 2) * HD]

    key_or_value(0, wk)
    for n in range(pieces):
        wait_copies(copies[n])
        at = held + n * depth
        multiply(x[:, at : at + depth], late.at[n], keep, send, True)
    wait_copies(copies[pieces])
    key_or_value(1, wv_here)
    encode(coded, lambda cols: send[:, cols], keep.shape[1], True)
    wait_copies(*copies[pieces + 1 :])


def project_first(blocks, perm, early, w_key, w_query, w_value, chunks):
    rows = perm.shape[0]
    depth = w_query.shape[0]
    qc, kc = w_query.shape[1] // chunks, w_key.shape[1]
    width = qc + 2 * HD
    pieces = 3
    out = jax.ShapeDtypeStruct((rows // 2, width), F32)
    coded = jax.ShapeDtypeStruct((rows // 2, coded_width(width, True)), jnp.int16)
    return pl.pallas_call(
        functools.partial(first_kernel, len(blocks), chunks),
        name="project_first",
        in_specs=[IN_VMEM] * (len(blocks) + 3) + [ANYWHERE] * 2,
        out_specs=[IN_VMEM] * (2 + chunks + (chunks > 1)),
        out_shape=[out, coded, pltpu.VMEM((rows, depth), BF16)]
        + [jax.ShapeDtypeStruct((rows, 2 * HD), F32)] * (chunks - 1)
        + [pltpu.VMEM((depth // 8, qc), BF16)] * (chunks > 1),
        scratch_shapes=[
            pltpu.VMEM((rows // 2, width), F32),
            pltpu.VMEM((pieces, (depth - early.shape[0]) // pieces, qc), BF16),
            pltpu.VMEM((depth, kc), BF16),
            pltpu.VMEM((rows, depth), BF16),
            pltpu.SemaphoreType.DMA((pieces + 2, 8)),
        ],
        compiler_params=pltpu.CompilerParams(vmem_limit_bytes=16 * MIB),
        cost_estimate=pl.CostEstimate(
            flops=2 * rows * depth * width, bytes_accessed=4 * depth * width, transcendentals=0
        ),
    )(*blocks, perm, in_vmem(early), in_vmem(w_key), in_hbm(w_query), in_hbm(w_value))


def next_kernel(chunk, more, x, early, kv, wq, *refs):
    keep, coded = refs[:2]
    send, late, sems = refs[-3:]
    pieces, depth, qc = late.shape
    held = early.shape[0]
    copies = [
        copy_pieces(wq.at[pl.ds(held + n * depth, depth), pl.ds(chunk * qc, qc)], late.at[n], sems.at[n], 2)
        for n in range(pieces)
    ]
    if more:
        copies.append(
            copy_pieces(wq.at[pl.ds(0, held), pl.ds((chunk + 1) * qc, qc)], refs[2], sems.at[pieces], 4)
        )
    start_copies(*copies)
    put(keep, send, slice(qc, qc + 2 * HD), kv[...], False)
    multiply(x[:, :held], early, keep, send, False)
    for n in range(pieces):
        wait_copies(copies[n])
        at = held + n * depth
        multiply(x[:, at : at + depth], late.at[n], keep, send, True)
    encode(coded, lambda cols: send[:, cols], keep.shape[1], True)
    wait_copies(*copies[pieces:])


def project_next(x, early, kv, w_query, chunk, chunks):
    rows = x.shape[0]
    held, qc = early.shape
    pieces = 7
    depth = (x.shape[1] - held) // pieces
    width = qc + 2 * HD
    more = chunk + 1 < chunks
    out = jax.ShapeDtypeStruct((rows // 2, width), F32)
    coded = jax.ShapeDtypeStruct((rows // 2, coded_width(width, True)), jnp.int16)
    return pl.pallas_call(
        functools.partial(next_kernel, chunk, more),
        name=f"project_next_{chunk}",
        in_specs=[IN_VMEM] * 3 + [ANYWHERE],
        out_specs=[IN_VMEM] * (2 + more),
        out_shape=[out, coded] + [pltpu.VMEM(early.shape, BF16)] * more,
        scratch_shapes=[
            pltpu.VMEM((rows // 2, width), F32),
            pltpu.VMEM((pieces, depth, qc), BF16),
            pltpu.SemaphoreType.DMA((pieces + 1, 8)),
        ],
        compiler_params=pltpu.CompilerParams(vmem_limit_bytes=16 * MIB),
        cost_estimate=pl.CostEstimate(
            flops=2 * rows * x.shape[1] * width, bytes_accessed=4 * x.shape[1] * width, transcendentals=0
        ),
    )(x, in_vmem(early), kv, in_hbm(w_query))


def attend_kernel(count, heads, joined, groups, lengths, *refs):
    blocks, (cosine, sine, keys, values), refs = refs[:count], refs[count : count + 4], refs[count + 4 :]
    before, targets, refs = refs[:joined], refs[joined : joined + count], refs[joined + count :]
    packed, staged, scores, weights_low, mixed = refs
    rows = blocks[0].shape[0]
    pairs = count * rows
    slots = keys.shape[1]
    query_cols = heads * HD
    scale = 1.0 / jnp.sqrt(jnp.float32(HD))
    cos, sin = cosine[...], sine[...]

    def rotated(u):
        return u * cos + pltpu.roll(u, HD // 2, 1) * sin

    for k in range(count):
        packed[k * rows : (k + 1) * rows, :] = blocks[k][...].astype(F32)
    for h in range(heads):
        staged[:, h, :] = rotated(packed[:, h * HD : (h + 1) * HD])
    key_rot = rotated(packed[:, query_cols : query_cols + HD]).astype(BF16).astype(F32)
    slot = lax.broadcasted_iota(jnp.int32, (heads, slots), 1)

    def lanes(k):
        return pl.ds(pl.multiple_of(groups[k] * HD, HD), HD)

    for p in range(pairs):
        k, r = divmod(p, rows)
        scores[p] = lax.dot_general(
            staged[p].astype(BF16), keys[r, :, lanes(k)], (((1,), (1,)), ((), ())), preferred_element_type=F32
        )
    owns, denominators = [], []
    for p in range(pairs):
        r = p % rows
        q = staged[p].astype(BF16).astype(F32)
        masked = jnp.where(slot < lengths[r], scores[p] * scale, -jnp.inf)
        own = jnp.sum(q * key_rot[p : p + 1], axis=1, keepdims=True) * scale
        highest = jnp.maximum(jnp.max(masked, axis=1, keepdims=True), own)
        weights = jnp.exp(masked - highest)
        own_weight = jnp.exp(own - highest)
        denominators.append(jnp.sum(weights, axis=1, keepdims=True) + own_weight)
        owns.append(own_weight.astype(BF16).astype(F32))
        weights_low[p] = weights.astype(BF16)
    for p in range(pairs):
        k, r = divmod(p, rows)
        mixture = jnp.dot(weights_low[p], values[r, :, lanes(k)], preferred_element_type=F32)
        mixture = mixture + owns[p] * packed[p : p + 1, query_cols + HD :]
        mixed[p] = mixture / denominators[p]
    at = 0
    if joined:
        at = before[0].shape[1]
        for target, done in zip(targets, before):
            target[:, :at] = done[...]
    for h in range(heads):
        low = mixed[:, h, :].astype(BF16)
        for k, target in enumerate(targets):
            target[:, at + h * HD : at + (h + 1) * HD] = low[k * rows : (k + 1) * rows]


def attend(blocks, groups, lengths, cosine, sine, cache_keys, cache_values, before):
    rows, width = blocks[0].shape
    heads = (width - 2 * HD) // HD
    count = len(blocks)
    pairs = count * rows
    slots = cache_keys.shape[1]
    done = before[0].shape[1] if before else 0
    out = jax.ShapeDtypeStruct((rows, done + heads * HD), BF16)
    return pl.pallas_call(
        functools.partial(attend_kernel, count, heads, len(before)),
        name=f"attend_{done // (heads * HD)}",
        in_specs=[IN_SMEM, IN_SMEM] + [IN_VMEM] * (count + 4 + len(before)),
        out_specs=[IN_VMEM] * count,
        out_shape=[out] * count,
        scratch_shapes=[
            pltpu.VMEM((pairs, width), F32),
            pltpu.VMEM((pairs, heads, HD), F32),
            pltpu.VMEM((pairs, heads, slots), F32),
            pltpu.VMEM((pairs, heads, slots), BF16),
            pltpu.VMEM((pairs, heads, HD), F32),
        ],
        compiler_params=pltpu.CompilerParams(vmem_limit_bytes=8 * MIB),
        cost_estimate=pl.CostEstimate(
            flops=4 * pairs * heads * HD * slots, bytes_accessed=4 * rows * slots * count * HD, transcendentals=0
        ),
    )(groups, lengths, *blocks, cosine, sine, in_vmem(cache_keys), in_vmem(cache_values), *before)


def gather_rows(blocks, perm, gathered, x):
    rows = blocks[0].shape[0]
    for k, block in enumerate(blocks):
        gathered[k * rows : (k + 1) * rows, :] = block[...]
    tile = tile_of(x.shape[1])
    for at in range(0, x.shape[1], tile):
        x[:, at : at + tile] = jnp.dot(
            perm[...], gathered[:, at : at + tile], preferred_element_type=F32
        ).astype(BF16)


def columns(x, weights, cols):
    at, product = 0, None
    for w in weights:
        term = jnp.dot(x[:, at : at + w.shape[0]], w[:, cols], preferred_element_type=F32)
        product = term if product is None else product + term
        at += w.shape[0]
    return product


def early_kernel(count, held, first, *refs):
    blocks, perm, weights, refs = refs[:count], refs[count], refs[count + 1 : count + 1 + held], refs[count + 1 + held :]
    w, total, ahead, gathered, x, sems = refs
    copy = copy_pieces(w.at[pl.ds(first, ahead.shape[0])], ahead, sems)
    start_copies(copy)
    gather_rows(blocks, perm, gathered, x)
    tile = tile_of(total.shape[1])
    for n in range(0, total.shape[1], tile):
        total[:, n : n + tile] = columns(x, weights, slice(n, n + tile))
    wait_copies(copy)


def out_early(blocks, perm, weights, w_out, first):
    rows, size, width = perm.shape[0], blocks[0].shape[1], w_out.shape[1]
    return pl.pallas_call(
        functools.partial(early_kernel, len(blocks), len(weights), first),
        name="out_early",
        in_specs=[IN_VMEM] * (len(blocks) + 1 + len(weights)) + [ANYWHERE],
        out_specs=[IN_VMEM] * 2,
        out_shape=[pltpu.VMEM((rows, width), F32), pltpu.VMEM((w_out.shape[0] - first, width), BF16)],
        scratch_shapes=[
            pltpu.VMEM((rows, size), BF16),
            pltpu.VMEM((rows, size), BF16),
            pltpu.SemaphoreType.DMA((8,)),
        ],
        compiler_params=pltpu.CompilerParams(vmem_limit_bytes=6 * MIB),
        cost_estimate=pl.CostEstimate(
            flops=2 * rows * size * width, bytes_accessed=2 * size * width, transcendentals=0
        ),
    )(*blocks, perm, *[in_vmem(w) for w in weights], in_hbm(w_out))


def out_kernel(count, held, earlier, part, fresh, *refs):
    blocks, refs = refs[:count], refs[count:]
    weights, totals, refs = refs[:held], refs[held : held + earlier], refs[held + earlier :]
    if fresh:
        perm, keep, send, x, gathered = refs
        gather_rows(blocks, perm, gathered, x)
    else:
        (x,), (keep, send) = blocks, refs
    half, width = keep.shape
    tile = tile_of(width)
    for n in range(0, width, tile):
        cols = slice(n, n + tile)
        there = slice(part * width + n, part * width + n + tile)
        product = columns(x, weights, there)
        for total in totals:
            product = product + total[:, there]
        keep[:, cols] = product[:half]
        send[:, cols] = product[half:]


def out_project(blocks, weights, totals, part, parts, perm=None):
    fresh = perm is not None
    size = blocks[0].shape[1]
    rows = sum(b.shape[0] for b in blocks)
    width = weights[0].shape[1] // parts
    out = jax.ShapeDtypeStruct((rows // 2, width), F32)
    return pl.pallas_call(
        functools.partial(out_kernel, len(blocks), len(weights), len(totals), part, fresh),
        name=f"out_project_{part}",
        in_specs=[IN_VMEM] * (len(blocks) + len(weights) + len(totals) + fresh),
        out_specs=[IN_VMEM] * (2 + fresh),
        out_shape=[out, out] + [pltpu.VMEM((rows, size), BF16)] * fresh,
        scratch_shapes=[pltpu.VMEM((rows, size), BF16)] * fresh,
        compiler_params=pltpu.CompilerParams(vmem_limit_bytes=6 * MIB),
        cost_estimate=pl.CostEstimate(
            flops=2 * rows * size * width, bytes_accessed=2 * size * width, transcendentals=0
        ),
    )(*blocks, *[in_vmem(w) for w in weights], *[in_vmem(t) for t in totals], *([perm] if fresh else []))


def local(hidden, w_query, w_key, w_value, w_out, cache_keys, cache_values, lengths):
    nz, ny = lax.axis_size("gx"), lax.axis_size("gy")
    z, y = lax.axis_index("gx"), lax.axis_index("gy")
    rows_dev = lengths.shape[0]
    rows = rows_dev * nz * ny
    rows_y, rows_z = rows // ny, rows // nz
    chunks = w_key.shape[1] // HD
    chunk_cols = w_query.shape[1] // chunks
    depth = w_query.shape[0]
    high_first = list(reversed(bit_list(ny)))

    kz, ky, i = np.meshgrid(halves_order(nz), np.arange(ny), np.arange(rows_dev), indexing="ij")
    kz, ky, i = (jnp.asarray(a.reshape(-1), jnp.int32) for a in (kz, ky, i))
    row = ((kz ^ z) * ny + (ky ^ y)) * rows_dev + i
    perm_in = one_hot(((row // rows_y) ^ y) * rows_y + row % rows_y, rows)
    ko, t = np.meshgrid(halves_order(ny), np.arange(rows_y), indexing="ij")
    ko, t = (jnp.asarray(a.reshape(-1), jnp.int32) for a in (ko, t))
    row = (ko ^ y) * rows_y + t
    from_z, rest = row // rows_z, row % rows_z
    perm_out = one_hot(
        ((from_z ^ z) * ny + ((rest // rows_dev) ^ y)) * rows_dev + rest % rows_dev, rows
    )

    frequency = 500000.0 ** (-(jnp.arange(HD // 2, dtype=F32) * 2.0) / HD)
    angles = lengths.astype(F32)[:, None] * frequency[None, :]
    cosine, sine = jnp.cos(angles), jnp.sin(angles)
    cosine = jnp.tile(jnp.concatenate([cosine, cosine], axis=1), (ny, 1))
    sine = jnp.tile(jnp.concatenate([-sine, sine], axis=1), (ny, 1))

    early_rows = depth * 10 // 16
    cols = pl.ds(0, chunk_cols)
    (w_first,) = fetch(
        "fetch_query",
        [after(w_query, z, y)],
        [(early_rows, chunk_cols)],
        [(0, (pl.ds(0, early_rows), cols), 0, (pl.ds(0, early_rows), cols))],
    )
    blocks = {0: hidden}
    far = high_first[0]
    for bit in high_first:
        blocks.update({k | bit: swap(b, "gy", bit) for k, b in list(blocks.items())})
        if bit == far:
            blocks[bit] = after(blocks[bit], w_first)
    whole_key = (pl.ds(0, depth), pl.ds(0, w_key.shape[1]))
    (w_key,) = fetch("fetch_key", [after(w_key, blocks[far])], [w_key.shape], [(0, whole_key, 0, whole_key)])
    blocks = [blocks[k] for k in range(ny)]
    blocks[-1] = after(blocks[-1], w_key)

    keep, send, x, *rest = project_first(blocks, perm_in, w_first, w_key, w_query, w_value, chunks)
    projected = [(keep, send)]
    for c in range(1, chunks):
        keep, send, *ahead = project_next(x, rest[-1], rest[c - 1], w_query, c, chunks)
        rest[-1:] = ahead
        projected.append((keep, send))

    sixteenth = w_out.shape[0] // 16

    def fetch_out(first, last, sent, others=()):
        shapes = [((last - first) * sixteenth, w_out.shape[1])] + [a.shape for a in others]
        window = (pl.ds(first * sixteenth, shapes[0][0]), pl.ds(0, shapes[0][1]))
        plan = [(0, window, 0, tuple(pl.ds(0, n) for n in shapes[0]))]
        for n, a in enumerate(others):
            whole = tuple(pl.ds(0, d) for d in a.shape)
            plan.append((n + 1, whole, n + 1, whole))
        return fetch(f"fetch_{first}_{last}", [after(w_out, sent), *others], shapes, plan)

    flying, sent = {}, {}
    for bit in bit_list(nz):
        for c in range(chunks):
            if bit == 1:
                keep, send = projected[c]
            else:
                keep, send = pass_on(f"pass_on_{c}_{bit}", flying[c][1], flying[c][0], True)
            flying[c] = (keep, swap(send, "gx", bit))
            sent[c] = send
            if bit == 2 and c == 0:
                w_0, keys, values = fetch_out(0, 4, send, (cache_keys, cache_values))
                last = chunks - 1
                flying[last] = (flying[last][0], after(flying[last][1], w_0, keys, values))

    heads_of = []
    for c in range(chunks):
        keep, arrived = flying[c]
        if c == 1:
            arrived = after(arrived, w_1)
        sent = finish_rows(f"finish_rows_{c}", arrived, keep, ny)
        parts = exchange(sent)
        if c == 0:
            (w_1,) = fetch_out(4, 8, sent[-1])
            parts[-1] = after(parts[-1], w_1)
        heads_of.append((sent, parts))
    before = ()
    for c, (_, parts) in enumerate(heads_of):
        if before:
            parts[-1] = after(parts[-1], before[-1])
        if c + 1 < chunks:
            parts[-1] = after(parts[-1], heads_of[c + 1][0][-1])
        groups = (jnp.arange(ny, dtype=jnp.int32) ^ y) * chunks + c
        before = attend(parts, groups, lengths, cosine, sine, keys, values, before)
    (w_2,) = fetch_out(8, 12, before[-1])
    parts = exchange(before)
    parts[-1] = after(parts[-1], w_2)
    mine = jnp.concatenate(parts, axis=0)
    parts = [mine[:, c * chunk_cols : (c + 1) * chunk_cols] for c in range(chunks)]
    received = [[part] for part in parts]
    for k in range(1, nz):
        for c, part in enumerate(parts):
            received[c].append(swap(part, "gx", k))
    totals = []
    if chunks == 2:
        total, w_3 = out_early(received[0], perm_out, [w_0, w_1], w_out, 12 * sixteenth)
        weights, totals = [w_2, w_3], [total]
    else:
        (w_3,) = fetch_out(12, 16, mine)
        received[-1][-1] = after(received[-1][-1], w_3)
        weights = [w_0, w_1, w_2, w_3]

    pieces = 2
    arrived, keeps = [], []
    for part in range(pieces):
        if part == 0:
            keep, send, x = out_project(received[-1], weights, totals, part, pieces, perm_out)
        else:
            keep, send = out_project([x], weights, totals, part, pieces)
        for bit in bit_list(ny)[1:]:
            keep, send = pass_on(f"out_pass_{part}_{bit}", swap(send, "gy", bit // 2), keep, False)
        keeps.append(keep)
        arrived.append(swap(send, "gy", far))
    return finish_out(arrived, keeps)


def solution(mesh):
    placed = (
        P(("groups", "gy"), "gx"),
        P("gx", "gy"),
        P("gx", "gy"),
        P("gx", "gy"),
        P("gy", "gx"),
        P(("groups", "gx", "gy"), None, None),
        P(("groups", "gx", "gy"), None, None),
        P(("groups", "gx", "gy")),
    )
    return jax.shard_map(
        local, mesh=mesh, in_specs=placed, out_specs=P(("groups", "gy"), "gx"), check_vma=False
    )
```

```python
import functools

import jax
import jax.numpy as jnp
import numpy as np
from jax import lax
from jax.experimental import pallas as pl
from jax.experimental.pallas import tpu as pltpu
from jax.sharding import PartitionSpec as P

HD = 128
MIB = 1 << 20
F32 = jnp.float32
BF16 = jnp.bfloat16


def swap(x, axis, offset):
    n = lax.axis_size(axis)
    return lax.ppermute(x, axis, [(i, i ^ offset) for i in range(n)])


def bit_list(n):
    return [1 << b for b in range(n.bit_length() - 1)]


def halves_order(n):
    bits = bit_list(n)
    out = []
    for position in range(n):
        k = 0
        for level, bit in enumerate(bits):
            if position >> (len(bits) - 1 - level) & 1:
                k |= bit
        out.append(k)
    return np.array(out)


def exchange(parts):
    return [parts[0]] + [swap(parts[k], "gy", k) for k in range(1, len(parts))]


def one_hot(columns, size):
    return (columns[:, None] == jnp.arange(size, dtype=jnp.int32)[None, :]).astype(BF16)


def in_hbm(x):
    return pltpu.with_memory_space_constraint(x, pltpu.HBM)


def in_vmem(x):
    return pltpu.with_memory_space_constraint(x, pltpu.VMEM)


ANYWHERE = pl.BlockSpec(memory_space=pl.ANY)
IN_VMEM = pl.BlockSpec(memory_space=pltpu.VMEM)
IN_SMEM = pl.BlockSpec(memory_space=pltpu.SMEM)


def row_pieces(rows, wanted):
    pieces = wanted
    while rows % pieces or (rows >= 16 * pieces and (rows // pieces) % 16):
        pieces //= 2
    return pieces


def copy_pieces(source, target, sems, wanted=8):
    pieces = row_pieces(target.shape[0], wanted)
    step = target.shape[0] // pieces

    def piece(n):
        at = pl.ds(pl.multiple_of(n * step, step), step)
        return pltpu.make_async_copy(source.at[at], target.at[at], sems.at[n])

    return pieces, piece


def start_copies(*copies):
    for pieces, piece in copies:
        pl.loop(0, pieces)(lambda n: piece(n).start())


def wait_copies(*copies):
    for pieces, piece in copies:
        pl.loop(0, pieces)(lambda n: piece(n).wait())


def fetch_kernel(plan, count, *refs):
    sources, targets, sems = refs[:count], refs[count:-1], refs[-1]
    copies = [
        copy_pieces(sources[source].at[window], targets[target].at[place], sems.at[n])
        for n, (source, window, target, place) in enumerate(plan)
    ]
    start_copies(*copies)
    wait_copies(*copies)


def fetch(name, arrays, shapes, plan):
    return pl.pallas_call(
        functools.partial(fetch_kernel, plan, len(arrays)),
        name=name,
        in_specs=[ANYWHERE] * len(arrays),
        out_specs=[IN_VMEM] * len(shapes),
        out_shape=[pltpu.VMEM(shape, BF16) for shape in shapes],
        scratch_shapes=[pltpu.SemaphoreType.DMA((len(plan), 8))],
        compiler_params=pltpu.CompilerParams(vmem_limit_bytes=MIB),
        cost_estimate=pl.CostEstimate(
            flops=0, bytes_accessed=2 * sum(int(np.prod(shape)) for shape in shapes), transcendentals=0
        ),
    )(*[in_hbm(a) for a in arrays])


def after(x, *done):
    return lax.optimization_barrier((x, *done))[0]


def tile_of(width, wanted=512):
    return wanted if width % wanted == 0 else width


FINE, COARSE = 8372224.0, 32752.0


def coded_width(cols, fine):
    return cols + (cols // 2 if fine else 0) + HD


def encode(coded, value, cols, fine):
    lane = lax.broadcasted_iota(jnp.int32, (coded.shape[0], HD), 1)
    exponents = jnp.zeros(lane.shape, jnp.int32)
    lower = None
    for g in range(cols // HD):
        v = value(slice(g * HD, (g + 1) * HD))
        largest = jnp.max(jnp.abs(v), axis=1, keepdims=True)
        exponent = jnp.maximum(jnp.ceil(jnp.log2(jnp.maximum(largest, 1e-31))), -100.0)
        n = jnp.floor(v * ((FINE if fine else COARSE) / jnp.exp2(exponent)) + 0.5).astype(jnp.int32)
        exponents = jnp.where(lane == g, exponent.astype(jnp.int32), exponents)
        if fine:
            coded[:, g * HD : (g + 1) * HD] = (n >> 8).astype(jnp.int16)
            if g % 2 == 0:
                lower = n & 255
            else:
                both = lower * 256 + (n & 255) - 32768
                coded[:, cols + g // 2 * HD : cols + (g // 2 + 1) * HD] = both.astype(jnp.int16)
        else:
            coded[:, g * HD : (g + 1) * HD] = n.astype(jnp.int16)
    coded[:, coded.shape[1] - HD :] = exponents.astype(jnp.int16)


def decode(coded, cols, fine):
    scales = jnp.exp2(coded[:, coded.shape[1] - HD :].astype(F32)) / (FINE if fine else COARSE)
    for g in range(cols // HD):
        n = coded[:, g * HD : (g + 1) * HD].astype(jnp.int32)
        if fine:
            if g % 2 == 0:
                both = coded[:, cols + g // 2 * HD : cols + (g // 2 + 1) * HD].astype(jnp.int32) + 32768
            n = n * 256 + ((both >> 8) if g % 2 == 0 else (both & 255))
        yield slice(g * HD, (g + 1) * HD), n.astype(F32) * scales[:, g : g + 1]


def pass_kernel(fine, coded_in, keep, *refs):
    if coded_in.dtype == jnp.int16:
        arrived = decode(coded_in, keep.shape[1], fine)
    else:
        arrived = ((slice(g, g + HD), coded_in[:, g : g + HD]) for g in range(0, keep.shape[1], HD))
    kept, coded_out, total = refs
    half = kept.shape[0]
    for cols, value in arrived:
        value = keep[:, cols] + value
        kept[:, cols] = value[:half]
        total[:, cols] = value[half:]
    encode(coded_out, lambda cols: total[:, cols], keep.shape[1], fine)


def pass_on(name, arrived, keep, fine):
    rows, cols = keep.shape[0] // 2, keep.shape[1]
    return pl.pallas_call(
        functools.partial(pass_kernel, fine),
        name=name,
        in_specs=[IN_VMEM] * 2,
        out_specs=[IN_VMEM] * 2,
        out_shape=[
            jax.ShapeDtypeStruct((rows, cols), F32),
            jax.ShapeDtypeStruct((rows, coded_width(cols, fine)), jnp.int16),
        ],
        scratch_shapes=[pltpu.VMEM((rows, cols), F32)],
        compiler_params=pltpu.CompilerParams(vmem_limit_bytes=6 * MIB),
        cost_estimate=pl.CostEstimate(flops=40 * rows * cols, bytes_accessed=16 * rows * cols, transcendentals=0),
    )(arrived, keep)


def finish_rows_kernel(coded, keep, *parts):
    rows = parts[0].shape[0]
    for cols, value in decode(coded, keep.shape[1], True):
        value = keep[:, cols] + value
        for n, part in enumerate(parts):
            part[:, cols] = value[n * rows : (n + 1) * rows].astype(BF16)


def finish_rows(name, arrived, keep, parts):
    rows, cols = keep.shape[0] // parts, keep.shape[1]
    return pl.pallas_call(
        finish_rows_kernel,
        name=name,
        in_specs=[IN_VMEM] * 2,
        out_specs=[IN_VMEM] * parts,
        out_shape=[jax.ShapeDtypeStruct((rows, cols), BF16)] * parts,
        compiler_params=pltpu.CompilerParams(vmem_limit_bytes=6 * MIB),
        cost_estimate=pl.CostEstimate(flops=20 * rows * cols, bytes_accessed=16 * rows * cols, transcendentals=0),
    )(arrived, keep)


def finish_out_kernel(count, *refs):
    coded, keeps, out = refs[:count], refs[count : 2 * count], refs[2 * count]
    at = 0
    for arrived, keep in zip(coded, keeps):
        width = keep.shape[1]
        for cols, value in decode(arrived, width, False):
            out[:, at + cols.start : at + cols.stop] = (keep[:, cols] + value).astype(BF16)
        at += width


def finish_out(arrived, keeps):
    rows, cols = keeps[0].shape[0], sum(k.shape[1] for k in keeps)
    return pl.pallas_call(
        functools.partial(finish_out_kernel, len(keeps)),
        name="finish_out",
        in_specs=[IN_VMEM] * (2 * len(keeps)),
        out_specs=IN_VMEM,
        out_shape=jax.ShapeDtypeStruct((rows, cols), BF16),
        compiler_params=pltpu.CompilerParams(vmem_limit_bytes=8 * MIB),
        cost_estimate=pl.CostEstimate(flops=20 * rows * cols, bytes_accessed=16 * rows * cols, transcendentals=0),
    )(*arrived, *keeps)


def put(keep, send, cols, product, more):
    half = keep.shape[0]
    if more:
        keep[:, cols] += product[:half]
        send[:, cols] += product[half:]
    else:
        keep[:, cols] = product[:half]
        send[:, cols] = product[half:]


def multiply(x, weights, keep, send, more):
    tile = tile_of(weights.shape[1])
    for n in range(0, weights.shape[1], tile):
        product = jnp.dot(x, weights[:, n : n + tile], preferred_element_type=F32)
        put(keep, send, slice(n, n + tile), product, more)


def first_kernel(count, chunks, *refs):
    blocks, refs = refs[:count], refs[count:]
    perm, early, wk, wq, wv, keep, coded, x = refs[:8]
    others, refs = refs[8 : 7 + chunks], refs[7 + chunks :]
    ahead, refs = (refs[:1], refs[1:]) if chunks > 1 else ((), refs)
    send, late, wv_here, gathered, sems = refs
    held = early.shape[0]
    pieces, depth, qc = late.shape
    copies = [
        copy_pieces(wq.at[pl.ds(held + n * depth, depth), pl.ds(0, qc)], late.at[n], sems.at[n], 2)
        for n in range(pieces)
    ]
    copies.append(copy_pieces(wv, wv_here, sems.at[pieces], 4))
    for w in ahead:
        copies.append(copy_pieces(wq.at[pl.ds(0, w.shape[0]), pl.ds(qc, qc)], w, sems.at[pieces + 1], 4))
    start_copies(*copies)
    rows = blocks[0].shape[0]
    for k in range(count):
        gathered[k * rows : (k + 1) * rows, :] = blocks[k][...]
    width = x.shape[1]
    tile = tile_of(width)
    for at in range(0, width, tile):
        x[:, at : at + tile] = jnp.dot(
            perm[...], gathered[:, at : at + tile], preferred_element_type=F32
        ).astype(BF16)
    multiply(x[:, :held], early, keep, send, False)

    def key_or_value(n, w):
        product = jnp.dot(x[...], w[...], preferred_element_type=F32)
        put(keep, send, slice(qc + n * HD, qc + (n + 1) * HD), product[:, :HD], False)
        for c, other in enumerate(others):
            other[:, n * HD : (n + 1) * HD] = product[:, (c + 1) * HD : (c + 2) * HD]

    for n in range(pieces):
        wait_copies(copies[n])
        at = held + n * depth
        multiply(x[:, at : at + depth], late.at[n], keep, send, True)
    wait_copies(copies[pieces])
    key_or_value(0, wk)
    key_or_value(1, wv_here)
    encode(coded, lambda cols: send[:, cols], keep.shape[1], True)
    wait_copies(*copies[pieces + 1 :])


def project_first(blocks, perm, early, w_key, w_query, w_value, chunks):
    rows = perm.shape[0]
    depth = w_query.shape[0]
    qc, kc = w_query.shape[1] // chunks, w_key.shape[1]
    width = qc + 2 * HD
    pieces = 2
    out = jax.ShapeDtypeStruct((rows // 2, width), F32)
    coded = jax.ShapeDtypeStruct((rows // 2, coded_width(width, True)), jnp.int16)
    return pl.pallas_call(
        functools.partial(first_kernel, len(blocks), chunks),
        name="project_first",
        in_specs=[IN_VMEM] * (len(blocks) + 3) + [ANYWHERE] * 2,
        out_specs=[IN_VMEM] * (2 + chunks + (chunks > 1)),
        out_shape=[out, coded, pltpu.VMEM((rows, depth), BF16)]
        + [jax.ShapeDtypeStruct((rows, 2 * HD), F32)] * (chunks - 1)
        + [pltpu.VMEM((depth // 4, qc), BF16)] * (chunks > 1),
        scratch_shapes=[
            pltpu.VMEM((rows // 2, width), F32),
            pltpu.VMEM((pieces, (depth - early.shape[0]) // pieces, qc), BF16),
            pltpu.VMEM((depth, kc), BF16),
            pltpu.VMEM((rows, depth), BF16),
            pltpu.SemaphoreType.DMA((pieces + 2, 8)),
        ],
        compiler_params=pltpu.CompilerParams(vmem_limit_bytes=16 * MIB),
        cost_estimate=pl.CostEstimate(
            flops=2 * rows * depth * width, bytes_accessed=4 * depth * width, transcendentals=0
        ),
    )(*blocks, perm, in_vmem(early), in_vmem(w_key), in_hbm(w_query), in_hbm(w_value))


def next_kernel(chunk, more, x, early, kv, wq, *refs):
    keep, coded = refs[:2]
    send, late, sems = refs[-3:]
    pieces, depth, qc = late.shape
    held = early.shape[0]
    copies = [
        copy_pieces(wq.at[pl.ds(held + n * depth, depth), pl.ds(chunk * qc, qc)], late.at[n], sems.at[n], 2)
        for n in range(pieces)
    ]
    if more:
        copies.append(
            copy_pieces(wq.at[pl.ds(0, held), pl.ds((chunk + 1) * qc, qc)], refs[2], sems.at[pieces], 4)
        )
    start_copies(*copies)
    put(keep, send, slice(qc, qc + 2 * HD), kv[...], False)
    multiply(x[:, :held], early, keep, send, False)
    for n in range(pieces):
        wait_copies(copies[n])
        at = held + n * depth
        multiply(x[:, at : at + depth], late.at[n], keep, send, True)
    encode(coded, lambda cols: send[:, cols], keep.shape[1], True)
    wait_copies(*copies[pieces:])


def project_next(x, early, kv, w_query, chunk, chunks):
    rows = x.shape[0]
    held, qc = early.shape
    pieces = 6
    depth = (x.shape[1] - held) // pieces
    width = qc + 2 * HD
    more = chunk + 1 < chunks
    out = jax.ShapeDtypeStruct((rows // 2, width), F32)
    coded = jax.ShapeDtypeStruct((rows // 2, coded_width(width, True)), jnp.int16)
    return pl.pallas_call(
        functools.partial(next_kernel, chunk, more),
        name=f"project_next_{chunk}",
        in_specs=[IN_VMEM] * 3 + [ANYWHERE],
        out_specs=[IN_VMEM] * (2 + more),
        out_shape=[out, coded] + [pltpu.VMEM(early.shape, BF16)] * more,
        scratch_shapes=[
            pltpu.VMEM((rows // 2, width), F32),
            pltpu.VMEM((pieces, depth, qc), BF16),
            pltpu.SemaphoreType.DMA((pieces + 1, 8)),
        ],
        compiler_params=pltpu.CompilerParams(vmem_limit_bytes=16 * MIB),
        cost_estimate=pl.CostEstimate(
            flops=2 * rows * x.shape[1] * width, bytes_accessed=4 * x.shape[1] * width, transcendentals=0
        ),
    )(x, in_vmem(early), kv, in_hbm(w_query))


def attend_kernel(count, heads, joined, groups, lengths, *refs):
    blocks, (cosine, sine, keys, values), refs = refs[:count], refs[count : count + 4], refs[count + 4 :]
    before, targets, refs = refs[:joined], refs[joined : joined + count], refs[joined + count :]
    packed, staged, scores, weights_low, mixed = refs
    rows = blocks[0].shape[0]
    pairs = count * rows
    slots = keys.shape[1]
    query_cols = heads * HD
    scale = 1.0 / jnp.sqrt(jnp.float32(HD))
    cos, sin = cosine[...], sine[...]

    def rotated(u):
        return u * cos + pltpu.roll(u, HD // 2, 1) * sin

    for k in range(count):
        packed[k * rows : (k + 1) * rows, :] = blocks[k][...].astype(F32)
    for h in range(heads):
        staged[:, h, :] = rotated(packed[:, h * HD : (h + 1) * HD])
    key_rot = rotated(packed[:, query_cols : query_cols + HD]).astype(BF16).astype(F32)
    slot = lax.broadcasted_iota(jnp.int32, (heads, slots), 1)

    def lanes(k):
        return pl.ds(pl.multiple_of(groups[k] * HD, HD), HD)

    for p in range(pairs):
        k, r = divmod(p, rows)
        scores[p] = lax.dot_general(
            staged[p].astype(BF16), keys[r, :, lanes(k)], (((1,), (1,)), ((), ())), preferred_element_type=F32
        )
    owns, denominators = [], []
    for p in range(pairs):
        r = p % rows
        q = staged[p].astype(BF16).astype(F32)
        masked = jnp.where(slot < lengths[r], scores[p] * scale, -jnp.inf)
        own = jnp.sum(q * key_rot[p : p + 1], axis=1, keepdims=True) * scale
        highest = jnp.maximum(jnp.max(masked, axis=1, keepdims=True), own)
        weights = jnp.exp(masked - highest)
        own_weight = jnp.exp(own - highest)
        denominators.append(jnp.sum(weights, axis=1, keepdims=True) + own_weight)
        owns.append(own_weight.astype(BF16).astype(F32))
        weights_low[p] = weights.astype(BF16)
    for p in range(pairs):
        k, r = divmod(p, rows)
        mixture = jnp.dot(weights_low[p], values[r, :, lanes(k)], preferred_element_type=F32)
        mixture = mixture + owns[p] * packed[p : p + 1, query_cols + HD :]
        mixed[p] = mixture / denominators[p]
    at = 0
    if joined:
        at = before[0].shape[1]
        for target, done in zip(targets, before):
            target[:, :at] = done[...]
    for h in range(heads):
        low = mixed[:, h, :].astype(BF16)
        for k, target in enumerate(targets):
            target[:, at + h * HD : at + (h + 1) * HD] = low[k * rows : (k + 1) * rows]


def attend(blocks, groups, lengths, cosine, sine, cache_keys, cache_values, before):
    rows, width = blocks[0].shape
    heads = (width - 2 * HD) // HD
    count = len(blocks)
    pairs = count * rows
    slots = cache_keys.shape[1]
    done = before[0].shape[1] if before else 0
    out = jax.ShapeDtypeStruct((rows, done + heads * HD), BF16)
    return pl.pallas_call(
        functools.partial(attend_kernel, count, heads, len(before)),
        name=f"attend_{done // (heads * HD)}",
        in_specs=[IN_SMEM, IN_SMEM] + [IN_VMEM] * (count + 4 + len(before)),
        out_specs=[IN_VMEM] * count,
        out_shape=[out] * count,
        scratch_shapes=[
            pltpu.VMEM((pairs, width), F32),
            pltpu.VMEM((pairs, heads, HD), F32),
            pltpu.VMEM((pairs, heads, slots), F32),
            pltpu.VMEM((pairs, heads, slots), BF16),
            pltpu.VMEM((pairs, heads, HD), F32),
        ],
        compiler_params=pltpu.CompilerParams(vmem_limit_bytes=8 * MIB),
        cost_estimate=pl.CostEstimate(
            flops=4 * pairs * heads * HD * slots, bytes_accessed=4 * rows * slots * count * HD, transcendentals=0
        ),
    )(groups, lengths, *blocks, cosine, sine, in_vmem(cache_keys), in_vmem(cache_values), *before)


def gather_rows(blocks, perm, gathered, x):
    rows = blocks[0].shape[0]
    for k, block in enumerate(blocks):
        gathered[k * rows : (k + 1) * rows, :] = block[...]
    tile = tile_of(x.shape[1])
    for at in range(0, x.shape[1], tile):
        x[:, at : at + tile] = jnp.dot(
            perm[...], gathered[:, at : at + tile], preferred_element_type=F32
        ).astype(BF16)


def columns(x, weights, cols):
    at, product = 0, None
    for w in weights:
        term = jnp.dot(x[:, at : at + w.shape[0]], w[:, cols], preferred_element_type=F32)
        product = term if product is None else product + term
        at += w.shape[0]
    return product


def early_kernel(count, held, first, *refs):
    blocks, perm, weights, refs = refs[:count], refs[count], refs[count + 1 : count + 1 + held], refs[count + 1 + held :]
    w, total, ahead, gathered, x, sems = refs
    copy = copy_pieces(w.at[pl.ds(first, ahead.shape[0])], ahead, sems)
    start_copies(copy)
    gather_rows(blocks, perm, gathered, x)
    tile = tile_of(total.shape[1])
    for n in range(0, total.shape[1], tile):
        total[:, n : n + tile] = columns(x, weights, slice(n, n + tile))
    wait_copies(copy)


def out_early(blocks, perm, weights, w_out, first):
    rows, size, width = perm.shape[0], blocks[0].shape[1], w_out.shape[1]
    return pl.pallas_call(
        functools.partial(early_kernel, len(blocks), len(weights), first),
        name="out_early",
        in_specs=[IN_VMEM] * (len(blocks) + 1 + len(weights)) + [ANYWHERE],
        out_specs=[IN_VMEM] * 2,
        out_shape=[pltpu.VMEM((rows, width), F32), pltpu.VMEM((w_out.shape[0] - first, width), BF16)],
        scratch_shapes=[
            pltpu.VMEM((rows, size), BF16),
            pltpu.VMEM((rows, size), BF16),
            pltpu.SemaphoreType.DMA((8,)),
        ],
        compiler_params=pltpu.CompilerParams(vmem_limit_bytes=6 * MIB),
        cost_estimate=pl.CostEstimate(
            flops=2 * rows * size * width, bytes_accessed=2 * size * width, transcendentals=0
        ),
    )(*blocks, perm, *[in_vmem(w) for w in weights], in_hbm(w_out))


def out_kernel(count, held, earlier, part, fresh, *refs):
    blocks, refs = refs[:count], refs[count:]
    weights, totals, refs = refs[:held], refs[held : held + earlier], refs[held + earlier :]
    if fresh:
        perm, keep, send, x, gathered = refs
        gather_rows(blocks, perm, gathered, x)
    else:
        (x,), (keep, send) = blocks, refs
    half, width = keep.shape
    tile = tile_of(width)
    for n in range(0, width, tile):
        cols = slice(n, n + tile)
        there = slice(part * width + n, part * width + n + tile)
        product = columns(x, weights, there)
        for total in totals:
            product = product + total[:, there]
        keep[:, cols] = product[:half]
        send[:, cols] = product[half:]


def out_project(blocks, weights, totals, part, parts, perm=None):
    fresh = perm is not None
    size = blocks[0].shape[1]
    rows = sum(b.shape[0] for b in blocks)
    width = weights[0].shape[1] // parts
    out = jax.ShapeDtypeStruct((rows // 2, width), F32)
    return pl.pallas_call(
        functools.partial(out_kernel, len(blocks), len(weights), len(totals), part, fresh),
        name=f"out_project_{part}",
        in_specs=[IN_VMEM] * (len(blocks) + len(weights) + len(totals) + fresh),
        out_specs=[IN_VMEM] * (2 + fresh),
        out_shape=[out, out] + [pltpu.VMEM((rows, size), BF16)] * fresh,
        scratch_shapes=[pltpu.VMEM((rows, size), BF16)] * fresh,
        compiler_params=pltpu.CompilerParams(vmem_limit_bytes=6 * MIB),
        cost_estimate=pl.CostEstimate(
            flops=2 * rows * size * width, bytes_accessed=2 * size * width, transcendentals=0
        ),
    )(*blocks, *[in_vmem(w) for w in weights], *[in_vmem(t) for t in totals], *([perm] if fresh else []))


def local(hidden, w_query, w_key, w_value, w_out, cache_keys, cache_values, lengths):
    nz, ny = lax.axis_size("gx"), lax.axis_size("gy")
    z, y = lax.axis_index("gx"), lax.axis_index("gy")
    rows_dev = lengths.shape[0]
    rows = rows_dev * nz * ny
    rows_y, rows_z = rows // ny, rows // nz
    chunks = w_key.shape[1] // HD
    chunk_cols = w_query.shape[1] // chunks
    depth = w_query.shape[0]
    high_first = list(reversed(bit_list(ny)))

    kz, ky, i = np.meshgrid(halves_order(nz), np.arange(ny), np.arange(rows_dev), indexing="ij")
    kz, ky, i = (jnp.asarray(a.reshape(-1), jnp.int32) for a in (kz, ky, i))
    row = ((kz ^ z) * ny + (ky ^ y)) * rows_dev + i
    perm_in = one_hot(((row // rows_y) ^ y) * rows_y + row % rows_y, rows)
    ko, t = np.meshgrid(halves_order(ny), np.arange(rows_y), indexing="ij")
    ko, t = (jnp.asarray(a.reshape(-1), jnp.int32) for a in (ko, t))
    row = (ko ^ y) * rows_y + t
    from_z, rest = row // rows_z, row % rows_z
    perm_out = one_hot(
        ((from_z ^ z) * ny + ((rest // rows_dev) ^ y)) * rows_dev + rest % rows_dev, rows
    )

    frequency = 500000.0 ** (-(jnp.arange(HD // 2, dtype=F32) * 2.0) / HD)
    angles = lengths.astype(F32)[:, None] * frequency[None, :]
    cosine, sine = jnp.cos(angles), jnp.sin(angles)
    cosine = jnp.tile(jnp.concatenate([cosine, cosine], axis=1), (ny, 1))
    sine = jnp.tile(jnp.concatenate([-sine, sine], axis=1), (ny, 1))

    early_rows = depth * 10 // 16
    cols = pl.ds(0, chunk_cols)
    (w_first,) = fetch(
        "fetch_query",
        [after(w_query, z, y)],
        [(early_rows, chunk_cols)],
        [(0, (pl.ds(0, early_rows), cols), 0, (pl.ds(0, early_rows), cols))],
    )
    blocks = {0: hidden}
    far = high_first[0]
    for bit in high_first:
        for k, block in list(blocks.items()):
            if bit != far and k == 0:
                block = after(block, w_first)
            blocks[k | bit] = swap(block, "gy", bit)
        if bit == far:
            blocks[bit] = after(blocks[bit], w_first)
    whole_key = (pl.ds(0, depth), pl.ds(0, w_key.shape[1]))
    (w_key,) = fetch("fetch_key", [after(w_key, blocks[far])], [w_key.shape], [(0, whole_key, 0, whole_key)])
    blocks = [blocks[k] for k in range(ny)]
    blocks[-1] = after(blocks[-1], w_key)

    keep, send, x, *rest = project_first(blocks, perm_in, w_first, w_key, w_query, w_value, chunks)
    projected = [(keep, send)]
    for c in range(1, chunks):
        keep, send, *ahead = project_next(x, rest[-1], rest[c - 1], w_query, c, chunks)
        rest[-1:] = ahead
        projected.append((keep, send))

    sixteenth = w_out.shape[0] // 16

    def fetch_out(first, last, sent, others=()):
        shapes = [((last - first) * sixteenth, w_out.shape[1])] + [a.shape for a in others]
        window = (pl.ds(first * sixteenth, shapes[0][0]), pl.ds(0, shapes[0][1]))
        plan = [(0, window, 0, tuple(pl.ds(0, n) for n in shapes[0]))]
        for n, a in enumerate(others):
            whole = tuple(pl.ds(0, d) for d in a.shape)
            plan.append((n + 1, whole, n + 1, whole))
        return fetch(f"fetch_{first}_{last}", [after(w_out, sent), *others], shapes, plan)

    flying, sent = {}, {}
    for bit in bit_list(nz):
        for c in range(chunks):
            if bit == 1:
                keep, send = projected[c]
            else:
                keep, send = pass_on(f"pass_on_{c}_{bit}", flying[c][1], flying[c][0], True)
            flying[c] = (keep, swap(send, "gx", bit))
            sent[c] = send
            if bit == 2 and c == 0:
                w_0, keys, values = fetch_out(0, 4, send, (cache_keys, cache_values))
                last = chunks - 1
                flying[last] = (flying[last][0], after(flying[last][1], w_0, keys, values))

    heads_of = []
    for c in range(chunks):
        keep, arrived = flying[c]
        if c == 1:
            arrived = after(arrived, w_1)
        sent = finish_rows(f"finish_rows_{c}", arrived, keep, ny)
        parts = exchange(sent)
        if c == 0:
            (w_1,) = fetch_out(4, 8, sent[-1])
            parts[-1] = after(parts[-1], w_1)
        heads_of.append((sent, parts))
    before = ()
    for c, (_, parts) in enumerate(heads_of):
        if before:
            parts[-1] = after(parts[-1], before[-1])
        if c + 1 < chunks:
            parts[-1] = after(parts[-1], heads_of[c + 1][0][-1])
        groups = (jnp.arange(ny, dtype=jnp.int32) ^ y) * chunks + c
        before = attend(parts, groups, lengths, cosine, sine, keys, values, before)
    (w_2,) = fetch_out(8, 12, before[-1])
    parts = exchange(before)
    parts[-1] = after(parts[-1], w_2)
    mine = jnp.concatenate(parts, axis=0)
    parts = [mine[:, c * chunk_cols : (c + 1) * chunk_cols] for c in range(chunks)]
    received = [[part] for part in parts]
    for k in range(1, nz):
        for c, part in enumerate(parts):
            received[c].append(swap(part, "gx", k))
    totals = []
    if chunks == 2:
        total, w_3 = out_early(received[0], perm_out, [w_0, w_1], w_out, 12 * sixteenth)
        weights, totals = [w_2, w_3], [total]
    else:
        (w_3,) = fetch_out(12, 16, mine)
        received[-1][-1] = after(received[-1][-1], w_3)
        weights = [w_0, w_1, w_2, w_3]

    pieces = 2
    arrived, keeps = [], []
    for part in range(pieces):
        if part == 0:
            keep, send, x = out_project(received[-1], weights, totals, part, pieces, perm_out)
        else:
            keep, send = out_project([x], weights, totals, part, pieces)
        for bit in bit_list(ny)[1:]:
            keep, send = pass_on(f"out_pass_{part}_{bit}", swap(send, "gy", bit // 2), keep, False)
        keeps.append(keep)
        arrived.append(swap(send, "gy", far))
    return finish_out(arrived, keeps)


def solution(mesh):
    placed = (
        P(("groups", "gy"), "gx"),
        P("gx", "gy"),
        P("gx", "gy"),
        P("gx", "gy"),
        P("gy", "gx"),
        P(("groups", "gx", "gy"), None, None),
        P(("groups", "gx", "gy"), None, None),
        P(("groups", "gx", "gy")),
    )
    return jax.shard_map(
        local, mesh=mesh, in_specs=placed, out_specs=P(("groups", "gy"), "gx"), check_vma=False
    )
```

```python
import functools

import jax
import jax.numpy as jnp
import numpy as np
from jax import lax
from jax.experimental import pallas as pl
from jax.experimental.pallas import tpu as pltpu
from jax.sharding import PartitionSpec as P

HD = 128
MIB = 1 << 20
F32 = jnp.float32
BF16 = jnp.bfloat16


def swap(x, axis, offset):
    n = lax.axis_size(axis)
    return lax.ppermute(x, axis, [(i, i ^ offset) for i in range(n)])


def bit_list(n):
    return [1 << b for b in range(n.bit_length() - 1)]


def halves_order(n):
    bits = bit_list(n)
    out = []
    for position in range(n):
        k = 0
        for level, bit in enumerate(bits):
            if position >> (len(bits) - 1 - level) & 1:
                k |= bit
        out.append(k)
    return np.array(out)


def exchange(parts):
    return [parts[0]] + [swap(parts[k], "gy", k) for k in range(1, len(parts))]


def one_hot(columns, size):
    return (columns[:, None] == jnp.arange(size, dtype=jnp.int32)[None, :]).astype(BF16)


def in_hbm(x):
    return pltpu.with_memory_space_constraint(x, pltpu.HBM)


def in_vmem(x):
    return pltpu.with_memory_space_constraint(x, pltpu.VMEM)


ANYWHERE = pl.BlockSpec(memory_space=pl.ANY)
IN_VMEM = pl.BlockSpec(memory_space=pltpu.VMEM)
IN_SMEM = pl.BlockSpec(memory_space=pltpu.SMEM)


def row_pieces(rows, wanted):
    pieces = wanted
    while rows % pieces or (rows >= 16 * pieces and (rows // pieces) % 16):
        pieces //= 2
    return pieces


def copy_pieces(source, target, sems, wanted=8):
    pieces = row_pieces(target.shape[0], wanted)
    step = target.shape[0] // pieces

    def piece(n):
        at = pl.ds(pl.multiple_of(n * step, step), step)
        return pltpu.make_async_copy(source.at[at], target.at[at], sems.at[n])

    return pieces, piece


def start_copies(*copies):
    for pieces, piece in copies:
        pl.loop(0, pieces)(lambda n: piece(n).start())


def wait_copies(*copies):
    for pieces, piece in copies:
        pl.loop(0, pieces)(lambda n: piece(n).wait())


def fetch_kernel(plan, count, *refs):
    sources, targets, sems = refs[:count], refs[count:-1], refs[-1]
    copies = [
        copy_pieces(sources[source].at[window], targets[target].at[place], sems.at[n])
        for n, (source, window, target, place) in enumerate(plan)
    ]
    start_copies(*copies)
    wait_copies(*copies)


def fetch(name, arrays, shapes, plan):
    return pl.pallas_call(
        functools.partial(fetch_kernel, plan, len(arrays)),
        name=name,
        in_specs=[ANYWHERE] * len(arrays),
        out_specs=[IN_VMEM] * len(shapes),
        out_shape=[pltpu.VMEM(shape, BF16) for shape in shapes],
        scratch_shapes=[pltpu.SemaphoreType.DMA((len(plan), 8))],
        compiler_params=pltpu.CompilerParams(vmem_limit_bytes=MIB),
        cost_estimate=pl.CostEstimate(
            flops=0, bytes_accessed=2 * sum(int(np.prod(shape)) for shape in shapes), transcendentals=0
        ),
    )(*[in_hbm(a) for a in arrays])


def after(x, *done):
    return lax.optimization_barrier((x, *done))[0]


def tile_of(width, wanted=512):
    return wanted if width % wanted == 0 else width


FINE, COARSE = 8372224.0, 32752.0


def coded_width(cols, fine):
    return cols + (cols // 2 if fine else 0) + HD


def encode(coded, value, cols, fine):
    lane = lax.broadcasted_iota(jnp.int32, (coded.shape[0], HD), 1)
    exponents = jnp.zeros(lane.shape, jnp.int32)
    lower = None
    for g in range(cols // HD):
        v = value(slice(g * HD, (g + 1) * HD))
        largest = jnp.max(jnp.abs(v), axis=1, keepdims=True)
        exponent = jnp.maximum(jnp.ceil(jnp.log2(jnp.maximum(largest, 1e-31))), -100.0)
        n = jnp.floor(v * ((FINE if fine else COARSE) / jnp.exp2(exponent)) + 0.5).astype(jnp.int32)
        exponents = jnp.where(lane == g, exponent.astype(jnp.int32), exponents)
        if fine:
            coded[:, g * HD : (g + 1) * HD] = (n >> 8).astype(jnp.int16)
            if g % 2 == 0:
                lower = n & 255
            else:
                both = lower * 256 + (n & 255) - 32768
                coded[:, cols + g // 2 * HD : cols + (g // 2 + 1) * HD] = both.astype(jnp.int16)
        else:
            coded[:, g * HD : (g + 1) * HD] = n.astype(jnp.int16)
    coded[:, coded.shape[1] - HD :] = exponents.astype(jnp.int16)


def decode(coded, cols, fine):
    scales = jnp.exp2(coded[:, coded.shape[1] - HD :].astype(F32)) / (FINE if fine else COARSE)
    for g in range(cols // HD):
        n = coded[:, g * HD : (g + 1) * HD].astype(jnp.int32)
        if fine:
            if g % 2 == 0:
                both = coded[:, cols + g // 2 * HD : cols + (g // 2 + 1) * HD].astype(jnp.int32) + 32768
            n = n * 256 + ((both >> 8) if g % 2 == 0 else (both & 255))
        yield slice(g * HD, (g + 1) * HD), n.astype(F32) * scales[:, g : g + 1]


def pass_kernel(fine, coded_in, keep, *refs):
    if coded_in.dtype == jnp.int16:
        arrived = decode(coded_in, keep.shape[1], fine)
    else:
        arrived = ((slice(g, g + HD), coded_in[:, g : g + HD]) for g in range(0, keep.shape[1], HD))
    kept, coded_out, total = refs
    half = kept.shape[0]
    for cols, value in arrived:
        value = keep[:, cols] + value
        kept[:, cols] = value[:half]
        total[:, cols] = value[half:]
    encode(coded_out, lambda cols: total[:, cols], keep.shape[1], fine)


def pass_on(name, arrived, keep, fine):
    rows, cols = keep.shape[0] // 2, keep.shape[1]
    return pl.pallas_call(
        functools.partial(pass_kernel, fine),
        name=name,
        in_specs=[IN_VMEM] * 2,
        out_specs=[IN_VMEM] * 2,
        out_shape=[
            jax.ShapeDtypeStruct((rows, cols), F32),
            jax.ShapeDtypeStruct((rows, coded_width(cols, fine)), jnp.int16),
        ],
        scratch_shapes=[pltpu.VMEM((rows, cols), F32)],
        compiler_params=pltpu.CompilerParams(vmem_limit_bytes=6 * MIB),
        cost_estimate=pl.CostEstimate(flops=40 * rows * cols, bytes_accessed=16 * rows * cols, transcendentals=0),
    )(arrived, keep)


def finish_rows_kernel(coded, keep, *parts):
    rows = parts[0].shape[0]
    for cols, value in decode(coded, keep.shape[1], True):
        value = keep[:, cols] + value
        for n, part in enumerate(parts):
            part[:, cols] = value[n * rows : (n + 1) * rows].astype(BF16)


def finish_rows(name, arrived, keep, parts):
    rows, cols = keep.shape[0] // parts, keep.shape[1]
    return pl.pallas_call(
        finish_rows_kernel,
        name=name,
        in_specs=[IN_VMEM] * 2,
        out_specs=[IN_VMEM] * parts,
        out_shape=[jax.ShapeDtypeStruct((rows, cols), BF16)] * parts,
        compiler_params=pltpu.CompilerParams(vmem_limit_bytes=6 * MIB),
        cost_estimate=pl.CostEstimate(flops=20 * rows * cols, bytes_accessed=16 * rows * cols, transcendentals=0),
    )(arrived, keep)


def finish_out_kernel(count, *refs):
    coded, keeps, out = refs[:count], refs[count : 2 * count], refs[2 * count]
    at = 0
    for arrived, keep in zip(coded, keeps):
        width = keep.shape[1]
        for cols, value in decode(arrived, width, False):
            out[:, at + cols.start : at + cols.stop] = (keep[:, cols] + value).astype(BF16)
        at += width


def finish_out(arrived, keeps):
    rows, cols = keeps[0].shape[0], sum(k.shape[1] for k in keeps)
    return pl.pallas_call(
        functools.partial(finish_out_kernel, len(keeps)),
        name="finish_out",
        in_specs=[IN_VMEM] * (2 * len(keeps)),
        out_specs=IN_VMEM,
        out_shape=jax.ShapeDtypeStruct((rows, cols), BF16),
        compiler_params=pltpu.CompilerParams(vmem_limit_bytes=8 * MIB),
        cost_estimate=pl.CostEstimate(flops=20 * rows * cols, bytes_accessed=16 * rows * cols, transcendentals=0),
    )(*arrived, *keeps)


def put(keep, send, cols, product, more):
    half = keep.shape[0]
    if more:
        keep[:, cols] += product[:half]
        send[:, cols] += product[half:]
    else:
        keep[:, cols] = product[:half]
        send[:, cols] = product[half:]


def multiply(x, weights, keep, send, more):
    tile = tile_of(weights.shape[1])
    for n in range(0, weights.shape[1], tile):
        product = jnp.dot(x, weights[:, n : n + tile], preferred_element_type=F32)
        put(keep, send, slice(n, n + tile), product, more)


def first_kernel(count, chunks, *refs):
    blocks, refs = refs[:count], refs[count:]
    perm, early, wk, wq, wv, keep, coded, x = refs[:8]
    others, refs = refs[8 : 7 + chunks], refs[7 + chunks :]
    ahead, refs = (refs[:1], refs[1:]) if chunks > 1 else ((), refs)
    send, late, wv_here, gathered, sems = refs
    held = early.shape[0]
    pieces, depth, qc = late.shape
    copies = [
        copy_pieces(wq.at[pl.ds(held + n * depth, depth), pl.ds(0, qc)], late.at[n], sems.at[n], 2)
        for n in range(pieces)
    ]
    copies.append(copy_pieces(wv, wv_here, sems.at[pieces], 4))
    for w in ahead:
        copies.append(copy_pieces(wq.at[pl.ds(0, w.shape[0]), pl.ds(qc, qc)], w, sems.at[pieces + 1], 4))
    start_copies(*copies)
    rows = blocks[0].shape[0]
    for k in range(count):
        gathered[k * rows : (k + 1) * rows, :] = blocks[k][...]
    width = x.shape[1]
    tile = tile_of(width)
    for at in range(0, width, tile):
        x[:, at : at + tile] = jnp.dot(
            perm[...], gathered[:, at : at + tile], preferred_element_type=F32
        ).astype(BF16)
    multiply(x[:, :held], early, keep, send, False)

    def key_or_value(n, w):
        product = jnp.dot(x[...], w[...], preferred_element_type=F32)
        put(keep, send, slice(qc + n * HD, qc + (n + 1) * HD), product[:, :HD], False)
        for c, other in enumerate(others):
            other[:, n * HD : (n + 1) * HD] = product[:, (c + 1) * HD : (c + 2) * HD]

    for n in range(pieces):
        wait_copies(copies[n])
        at = held + n * depth
        multiply(x[:, at : at + depth], late.at[n], keep, send, True)
    wait_copies(copies[pieces])
    key_or_value(0, wk)
    key_or_value(1, wv_here)
    encode(coded, lambda cols: send[:, cols], keep.shape[1], True)
    wait_copies(*copies[pieces + 1 :])


def project_first(blocks, perm, early, w_key, w_query, w_value, chunks):
    rows = perm.shape[0]
    depth = w_query.shape[0]
    qc, kc = w_query.shape[1] // chunks, w_key.shape[1]
    width = qc + 2 * HD
    pieces = 2
    out = jax.ShapeDtypeStruct((rows // 2, width), F32)
    coded = jax.ShapeDtypeStruct((rows // 2, coded_width(width, True)), jnp.int16)
    return pl.pallas_call(
        functools.partial(first_kernel, len(blocks), chunks),
        name="project_first",
        in_specs=[IN_VMEM] * (len(blocks) + 3) + [ANYWHERE] * 2,
        out_specs=[IN_VMEM] * (2 + chunks + (chunks > 1)),
        out_shape=[out, coded, pltpu.VMEM((rows, depth), BF16)]
        + [jax.ShapeDtypeStruct((rows, 2 * HD), F32)] * (chunks - 1)
        + [pltpu.VMEM((depth // 4, qc), BF16)] * (chunks > 1),
        scratch_shapes=[
            pltpu.VMEM((rows // 2, width), F32),
            pltpu.VMEM((pieces, (depth - early.shape[0]) // pieces, qc), BF16),
            pltpu.VMEM((depth, kc), BF16),
            pltpu.VMEM((rows, depth), BF16),
            pltpu.SemaphoreType.DMA((pieces + 2, 8)),
        ],
        compiler_params=pltpu.CompilerParams(vmem_limit_bytes=16 * MIB),
        cost_estimate=pl.CostEstimate(
            flops=2 * rows * depth * width, bytes_accessed=4 * depth * width, transcendentals=0
        ),
    )(*blocks, perm, in_vmem(early), in_vmem(w_key), in_hbm(w_query), in_hbm(w_value))


def next_kernel(chunk, more, x, early, kv, wq, *refs):
    keep, coded = refs[:2]
    send, late, sems = refs[-3:]
    pieces, depth, qc = late.shape
    held = early.shape[0]
    copies = [
        copy_pieces(wq.at[pl.ds(held + n * depth, depth), pl.ds(chunk * qc, qc)], late.at[n], sems.at[n], 2)
        for n in range(pieces)
    ]
    if more:
        copies.append(
            copy_pieces(wq.at[pl.ds(0, held), pl.ds((chunk + 1) * qc, qc)], refs[2], sems.at[pieces], 4)
        )
    start_copies(*copies)
    put(keep, send, slice(qc, qc + 2 * HD), kv[...], False)
    multiply(x[:, :held], early, keep, send, False)
    for n in range(pieces):
        wait_copies(copies[n])
        at = held + n * depth
        multiply(x[:, at : at + depth], late.at[n], keep, send, True)
    encode(coded, lambda cols: send[:, cols], keep.shape[1], True)
    wait_copies(*copies[pieces:])


def project_next(x, early, kv, w_query, chunk, chunks):
    rows = x.shape[0]
    held, qc = early.shape
    pieces = 6
    depth = (x.shape[1] - held) // pieces
    width = qc + 2 * HD
    more = chunk + 1 < chunks
    out = jax.ShapeDtypeStruct((rows // 2, width), F32)
    coded = jax.ShapeDtypeStruct((rows // 2, coded_width(width, True)), jnp.int16)
    return pl.pallas_call(
        functools.partial(next_kernel, chunk, more),
        name=f"project_next_{chunk}",
        in_specs=[IN_VMEM] * 3 + [ANYWHERE],
        out_specs=[IN_VMEM] * (2 + more),
        out_shape=[out, coded] + [pltpu.VMEM(early.shape, BF16)] * more,
        scratch_shapes=[
            pltpu.VMEM((rows // 2, width), F32),
            pltpu.VMEM((pieces, depth, qc), BF16),
            pltpu.SemaphoreType.DMA((pieces + 1, 8)),
        ],
        compiler_params=pltpu.CompilerParams(vmem_limit_bytes=16 * MIB),
        cost_estimate=pl.CostEstimate(
            flops=2 * rows * x.shape[1] * width, bytes_accessed=4 * x.shape[1] * width, transcendentals=0
        ),
    )(x, in_vmem(early), kv, in_hbm(w_query))


def attend_kernel(count, heads, joined, groups, lengths, *refs):
    blocks, (cosine, sine, keys, values), refs = refs[:count], refs[count : count + 4], refs[count + 4 :]
    before, targets, refs = refs[:joined], refs[joined : joined + count], refs[joined + count :]
    packed, staged, scores, weights_low, mixed = refs
    rows = blocks[0].shape[0]
    pairs = count * rows
    slots = keys.shape[1]
    query_cols = heads * HD
    scale = 1.0 / jnp.sqrt(jnp.float32(HD))
    cos, sin = cosine[...], sine[...]

    def rotated(u):
        return u * cos + pltpu.roll(u, HD // 2, 1) * sin

    for k in range(count):
        packed[k * rows : (k + 1) * rows, :] = blocks[k][...].astype(F32)
    for h in range(heads):
        staged[:, h, :] = rotated(packed[:, h * HD : (h + 1) * HD])
    key_rot = rotated(packed[:, query_cols : query_cols + HD]).astype(BF16).astype(F32)
    slot = lax.broadcasted_iota(jnp.int32, (heads, slots), 1)

    def lanes(k):
        return pl.ds(pl.multiple_of(groups[k] * HD, HD), HD)

    for p in range(pairs):
        k, r = divmod(p, rows)
        scores[p] = lax.dot_general(
            staged[p].astype(BF16), keys[r, :, lanes(k)], (((1,), (1,)), ((), ())), preferred_element_type=F32
        )
    owns, denominators = [], []
    for p in range(pairs):
        r = p % rows
        q = staged[p].astype(BF16).astype(F32)
        masked = jnp.where(slot < lengths[r], scores[p] * scale, -jnp.inf)
        own = jnp.sum(q * key_rot[p : p + 1], axis=1, keepdims=True) * scale
        highest = jnp.maximum(jnp.max(masked, axis=1, keepdims=True), own)
        weights = jnp.exp(masked - highest)
        own_weight = jnp.exp(own - highest)
        denominators.append(jnp.sum(weights, axis=1, keepdims=True) + own_weight)
        owns.append(own_weight.astype(BF16).astype(F32))
        weights_low[p] = weights.astype(BF16)
    for p in range(pairs):
        k, r = divmod(p, rows)
        mixture = jnp.dot(weights_low[p], values[r, :, lanes(k)], preferred_element_type=F32)
        mixture = mixture + owns[p] * packed[p : p + 1, query_cols + HD :]
        mixed[p] = mixture / denominators[p]
    at = 0
    if joined:
        at = before[0].shape[1]
        for target, done in zip(targets, before):
            target[:, :at] = done[...]
    for h in range(heads):
        low = mixed[:, h, :].astype(BF16)
        for k, target in enumerate(targets):
            target[:, at + h * HD : at + (h + 1) * HD] = low[k * rows : (k + 1) * rows]


def attend(blocks, groups, lengths, cosine, sine, cache_keys, cache_values, before):
    rows, width = blocks[0].shape
    heads = (width - 2 * HD) // HD
    count = len(blocks)
    pairs = count * rows
    slots = cache_keys.shape[1]
    done = before[0].shape[1] if before else 0
    out = jax.ShapeDtypeStruct((rows, done + heads * HD), BF16)
    return pl.pallas_call(
        functools.partial(attend_kernel, count, heads, len(before)),
        name=f"attend_{done // (heads * HD)}",
        in_specs=[IN_SMEM, IN_SMEM] + [IN_VMEM] * (count + 4 + len(before)),
        out_specs=[IN_VMEM] * count,
        out_shape=[out] * count,
        scratch_shapes=[
            pltpu.VMEM((pairs, width), F32),
            pltpu.VMEM((pairs, heads, HD), F32),
            pltpu.VMEM((pairs, heads, slots), F32),
            pltpu.VMEM((pairs, heads, slots), BF16),
            pltpu.VMEM((pairs, heads, HD), F32),
        ],
        compiler_params=pltpu.CompilerParams(vmem_limit_bytes=8 * MIB),
        cost_estimate=pl.CostEstimate(
            flops=4 * pairs * heads * HD * slots, bytes_accessed=4 * rows * slots * count * HD, transcendentals=0
        ),
    )(groups, lengths, *blocks, cosine, sine, in_vmem(cache_keys), in_vmem(cache_values), *before)


def gather_rows(blocks, perm, gathered, x):
    rows = blocks[0].shape[0]
    for k, block in enumerate(blocks):
        gathered[k * rows : (k + 1) * rows, :] = block[...]
    tile = tile_of(x.shape[1])
    for at in range(0, x.shape[1], tile):
        x[:, at : at + tile] = jnp.dot(
            perm[...], gathered[:, at : at + tile], preferred_element_type=F32
        ).astype(BF16)


def columns(x, weights, cols):
    at, product = 0, None
    for w in weights:
        term = jnp.dot(x[:, at : at + w.shape[0]], w[:, cols], preferred_element_type=F32)
        product = term if product is None else product + term
        at += w.shape[0]
    return product


def early_kernel(count, held, first, *refs):
    blocks, perm, weights, refs = refs[:count], refs[count], refs[count + 1 : count + 1 + held], refs[count + 1 + held :]
    w, total, ahead, gathered, x, sems = refs
    copy = copy_pieces(w.at[pl.ds(first, ahead.shape[0])], ahead, sems)
    start_copies(copy)
    gather_rows(blocks, perm, gathered, x)
    tile = tile_of(total.shape[1])
    for n in range(0, total.shape[1], tile):
        total[:, n : n + tile] = columns(x, weights, slice(n, n + tile))
    wait_copies(copy)


def out_early(blocks, perm, weights, w_out, first):
    rows, size, width = perm.shape[0], blocks[0].shape[1], w_out.shape[1]
    return pl.pallas_call(
        functools.partial(early_kernel, len(blocks), len(weights), first),
        name="out_early",
        in_specs=[IN_VMEM] * (len(blocks) + 1 + len(weights)) + [ANYWHERE],
        out_specs=[IN_VMEM] * 2,
        out_shape=[pltpu.VMEM((rows, width), F32), pltpu.VMEM((w_out.shape[0] - first, width), BF16)],
        scratch_shapes=[
            pltpu.VMEM((rows, size), BF16),
            pltpu.VMEM((rows, size), BF16),
            pltpu.SemaphoreType.DMA((8,)),
        ],
        compiler_params=pltpu.CompilerParams(vmem_limit_bytes=6 * MIB),
        cost_estimate=pl.CostEstimate(
            flops=2 * rows * size * width, bytes_accessed=2 * size * width, transcendentals=0
        ),
    )(*blocks, perm, *[in_vmem(w) for w in weights], in_hbm(w_out))


def out_kernel(count, held, earlier, part, fresh, *refs):
    blocks, refs = refs[:count], refs[count:]
    weights, totals, refs = refs[:held], refs[held : held + earlier], refs[held + earlier :]
    if fresh:
        perm, keep, send, x, gathered = refs
        gather_rows(blocks, perm, gathered, x)
    else:
        (x,), (keep, send) = blocks, refs
    half, width = keep.shape
    tile = tile_of(width)
    for n in range(0, width, tile):
        cols = slice(n, n + tile)
        there = slice(part * width + n, part * width + n + tile)
        product = columns(x, weights, there)
        for total in totals:
            product = product + total[:, there]
        keep[:, cols] = product[:half]
        send[:, cols] = product[half:]


def out_project(blocks, weights, totals, part, parts, perm=None):
    fresh = perm is not None
    size = blocks[0].shape[1]
    rows = sum(b.shape[0] for b in blocks)
    width = weights[0].shape[1] // parts
    out = jax.ShapeDtypeStruct((rows // 2, width), F32)
    return pl.pallas_call(
        functools.partial(out_kernel, len(blocks), len(weights), len(totals), part, fresh),
        name=f"out_project_{part}",
        in_specs=[IN_VMEM] * (len(blocks) + len(weights) + len(totals) + fresh),
        out_specs=[IN_VMEM] * (2 + fresh),
        out_shape=[out, out] + [pltpu.VMEM((rows, size), BF16)] * fresh,
        scratch_shapes=[pltpu.VMEM((rows, size), BF16)] * fresh,
        compiler_params=pltpu.CompilerParams(vmem_limit_bytes=6 * MIB),
        cost_estimate=pl.CostEstimate(
            flops=2 * rows * size * width, bytes_accessed=2 * size * width, transcendentals=0
        ),
    )(*blocks, *[in_vmem(w) for w in weights], *[in_vmem(t) for t in totals], *([perm] if fresh else []))


def local(hidden, w_query, w_key, w_value, w_out, cache_keys, cache_values, lengths):
    nz, ny = lax.axis_size("gx"), lax.axis_size("gy")
    z, y = lax.axis_index("gx"), lax.axis_index("gy")
    rows_dev = lengths.shape[0]
    rows = rows_dev * nz * ny
    rows_y, rows_z = rows // ny, rows // nz
    chunks = w_key.shape[1] // HD
    chunk_cols = w_query.shape[1] // chunks
    depth = w_query.shape[0]
    high_first = list(reversed(bit_list(ny)))

    kz, ky, i = np.meshgrid(halves_order(nz), np.arange(ny), np.arange(rows_dev), indexing="ij")
    kz, ky, i = (jnp.asarray(a.reshape(-1), jnp.int32) for a in (kz, ky, i))
    row = ((kz ^ z) * ny + (ky ^ y)) * rows_dev + i
    perm_in = one_hot(((row // rows_y) ^ y) * rows_y + row % rows_y, rows)
    ko, t = np.meshgrid(halves_order(ny), np.arange(rows_y), indexing="ij")
    ko, t = (jnp.asarray(a.reshape(-1), jnp.int32) for a in (ko, t))
    row = (ko ^ y) * rows_y + t
    from_z, rest = row // rows_z, row % rows_z
    perm_out = one_hot(
        ((from_z ^ z) * ny + ((rest // rows_dev) ^ y)) * rows_dev + rest % rows_dev, rows
    )

    frequency = 500000.0 ** (-(jnp.arange(HD // 2, dtype=F32) * 2.0) / HD)
    angles = lengths.astype(F32)[:, None] * frequency[None, :]
    cosine, sine = jnp.cos(angles), jnp.sin(angles)
    cosine = jnp.tile(jnp.concatenate([cosine, cosine], axis=1), (ny, 1))
    sine = jnp.tile(jnp.concatenate([-sine, sine], axis=1), (ny, 1))

    early_rows = depth * 10 // 16
    cols = pl.ds(0, chunk_cols)
    (w_first,) = fetch(
        "fetch_query",
        [after(w_query, z, y)],
        [(early_rows, chunk_cols)],
        [(0, (pl.ds(0, early_rows), cols), 0, (pl.ds(0, early_rows), cols))],
    )
    blocks = {0: hidden}
    far = high_first[0]
    for bit in high_first:
        for k, block in list(blocks.items()):
            if bit != far and k == 0:
                block = after(block, w_first)
            blocks[k | bit] = swap(block, "gy", bit)
        if bit == far:
            blocks[bit] = after(blocks[bit], w_first)
    whole_key = (pl.ds(0, depth), pl.ds(0, w_key.shape[1]))
    (w_key,) = fetch("fetch_key", [after(w_key, blocks[far])], [w_key.shape], [(0, whole_key, 0, whole_key)])
    blocks = [blocks[k] for k in range(ny)]
    blocks[-1] = after(blocks[-1], w_key)

    keep, send, x, *rest = project_first(blocks, perm_in, w_first, w_key, w_query, w_value, chunks)
    projected = [(keep, send)]
    for c in range(1, chunks):
        keep, send, *ahead = project_next(x, rest[-1], rest[c - 1], w_query, c, chunks)
        rest[-1:] = ahead
        projected.append((keep, send))

    sixteenth = w_out.shape[0] // 16

    def fetch_out(first, last, sent, others=()):
        shapes = [((last - first) * sixteenth, w_out.shape[1])] + [a.shape for a in others]
        window = (pl.ds(first * sixteenth, shapes[0][0]), pl.ds(0, shapes[0][1]))
        plan = [(0, window, 0, tuple(pl.ds(0, n) for n in shapes[0]))]
        for n, a in enumerate(others):
            whole = tuple(pl.ds(0, d) for d in a.shape)
            plan.append((n + 1, whole, n + 1, whole))
        return fetch(f"fetch_{first}_{last}", [after(w_out, sent), *others], shapes, plan)

    flying, sent = {}, {}
    for bit in bit_list(nz):
        for c in range(chunks):
            if bit == 1:
                keep, send = projected[c]
            else:
                keep, send = pass_on(f"pass_on_{c}_{bit}", flying[c][1], flying[c][0], True)
            flying[c] = (keep, swap(send, "gx", bit))
            sent[c] = send
            if bit == 2 and c == 0:
                w_0, keys, values = fetch_out(0, 4, send, (cache_keys, cache_values))
                last = chunks - 1
                flying[last] = (flying[last][0], after(flying[last][1], w_0, keys, values))

    heads_of = []
    for c in range(chunks):
        keep, arrived = flying[c]
        if c == 1:
            arrived = after(arrived, w_1)
        sent = finish_rows(f"finish_rows_{c}", arrived, keep, ny)
        parts = exchange(sent)
        if c == 0:
            (w_1,) = fetch_out(4, 8, sent[-1])
            parts[-1] = after(parts[-1], w_1)
        heads_of.append((sent, parts))
    before = ()
    for c, (_, parts) in enumerate(heads_of):
        if before:
            parts[-1] = after(parts[-1], before[-1])
        if c + 1 < chunks:
            parts[-1] = after(parts[-1], heads_of[c + 1][0][-1])
        groups = (jnp.arange(ny, dtype=jnp.int32) ^ y) * chunks + c
        before = attend(parts, groups, lengths, cosine, sine, keys, values, before)
    (w_2,) = fetch_out(8, 11, before[-1])
    parts = exchange(before)
    parts[-1] = after(parts[-1], w_2)
    mine = jnp.concatenate(parts, axis=0)
    parts = [mine[:, c * chunk_cols : (c + 1) * chunk_cols] for c in range(chunks)]
    received = [[part] for part in parts]
    for k in range(1, nz):
        for c, part in enumerate(parts):
            received[c].append(swap(part, "gx", k))
    totals = []
    if chunks == 2:
        total, w_3 = out_early(received[0], perm_out, [w_0, w_1], w_out, 11 * sixteenth)
        weights, totals = [w_2, w_3], [total]
    else:
        (w_3,) = fetch_out(11, 16, mine)
        received[-1][-1] = after(received[-1][-1], w_3)
        weights = [w_0, w_1, w_2, w_3]

    pieces = 2
    arrived, keeps = [], []
    for part in range(pieces):
        if part == 0:
            keep, send, x = out_project(received[-1], weights, totals, part, pieces, perm_out)
        else:
            keep, send = out_project([x], weights, totals, part, pieces)
        for bit in bit_list(ny)[1:]:
            keep, send = pass_on(f"out_pass_{part}_{bit}", swap(send, "gy", bit // 2), keep, False)
        keeps.append(keep)
        arrived.append(swap(send, "gy", far))
    return finish_out(arrived, keeps)


def solution(mesh):
    placed = (
        P(("groups", "gy"), "gx"),
        P("gx", "gy"),
        P("gx", "gy"),
        P("gx", "gy"),
        P("gy", "gx"),
        P(("groups", "gx", "gy"), None, None),
        P(("groups", "gx", "gy"), None, None),
        P(("groups", "gx", "gy")),
    )
    return jax.shard_map(
        local, mesh=mesh, in_specs=placed, out_specs=P(("groups", "gy"), "gx"), check_vma=False
    )
```
